32 devices in a mesh: groups: 2 (over x), seq: 16 (over z, y, core).
Axes of the slice: x: 2, y: 2, z: 4, core: 2. Of those that a mesh axis runs over, the one named last changes fastest.
Arguments:
- ssm_inputs: bfloat16 [4096, 2048], P(('groups', 'seq')), parts along dimension 0, may hold values from -6 to 6
- state_write: bfloat16 [4096, 128], P(('groups', 'seq')), parts along dimension 0, may hold values from -6 to 6
- state_read: bfloat16 [4096, 128], P(('groups', 'seq')), parts along dimension 0, may hold values from -6 to 6
- decay_codes: int32 [4096, 32], P(('groups', 'seq')), parts along dimension 0, may hold values from 0 to 4095, as said below
- decay_rate: float32 [32], replicated, as said below
- queries: bfloat16 [2, 4096, 2048], P(None, ('groups', 'seq')), parts along dimension 1, may hold values from -6 to 6
- keys_values: bfloat16 [2, 4096, 512], P(None, ('groups', 'seq')), parts along dimension 1, may hold values from -6 to 6
- segment_ids: int32 [4096], P(('groups', 'seq')), parts along dimension 0, may hold values from 0 to 3, never falling along the last dimension, each value on 1 to 1024 neighbouring positions
Outputs:
- ssm_output: bfloat16 [4096, 2048], P(('groups', 'seq')), parts along dimension 0
- attn_output: bfloat16 [2, 4096, 2048], P(None, ('groups', 'seq')), parts along dimension 1
The draws below stay inside these ranges and needn't reach their ends.
There are 2 independent parts, one for each index of `groups`. The reference program is written for one: setup_inputs(seed, part) draws one part's arguments, and reference() takes and returns one part's arrays. A program takes and returns all parts, laid end to end along the dimension named above; an argument that names none is the same for every part. Nothing has to cross between parts.
Inputs may be any that keep to these rules, and one draw needn't show every extreme that they name: `decay_codes`: the low ten bits of a code scale a head's rate, the higher bits mark rare positions at which every head loses part of its state. `decay_rate`: every rate is positive.
All inputs are finite; a program needn't handle non-finite values.
Results may differ from the reference program's by a relative error of at most 0.0047.
Values may be sent and summed in bfloat16 or wider, within the bound.
No kernel may reach another device: no remote copies, remote signals or barrier semaphores. Data moves between devices by JAX's collectives and lax.ppermute only.
A program may use at most 192 MiB of HBM per device.

```python
import math
import jax
import jax.numpy as jnp
import numpy as np
from jax import lax

HEADS_SSM = 32
HEAD_SSM = 64
STATE = 128
Q_HEADS = 16
KV_HEADS = 4
HEAD = 128
WINDOW = 1024
TOK_DEV = 128
TOKENS = 2048
N_SEQ = 16


def draw_decay_codes(key, part):
    first, second, third, fourth = jax.random.split(key, 4)
    blocks = TOKENS // TOK_DEV
    ceiling = jax.random.randint(first, (blocks, 1, 1), 64, 1024)
    lower = jax.random.randint(second, (blocks, TOK_DEV, HEADS_SSM), 0, ceiling + 1)
    lower = lower.reshape(TOKENS, HEADS_SSM)
    spots = jax.random.randint(third, (3,), 0, TOKENS)
    levels = jnp.array([3, 2, 2], jnp.int32) + jax.random.randint(fourth, (3,), 0, 2) * jnp.array([0, 1, 1], jnp.int32)
    positions = jnp.arange(TOKENS, dtype=jnp.int32)
    hits = positions[:, None] == spots[None, :]
    level = jnp.max(jnp.where(hits, levels[None, :], 0), axis=1)
    lower = jnp.where((level > 0)[:, None], 1023, lower)
    return (lower + 1024 * level[:, None]).astype(jnp.int32)


def draw_decay_rate(key, part):
    first, second, third = jax.random.split(key, 3)
    ranks = jax.random.permutation(first, HEADS_SSM)
    quick_heads = ranks < HEADS_SSM // 2
    quick = jnp.exp(jax.random.uniform(second, (HEADS_SSM,), minval=math.log(0.01), maxval=math.log(0.03)))
    slow = jnp.exp(jax.random.uniform(third, (HEADS_SSM,), minval=math.log(0.1), maxval=0.0)) / (8.0 * TOKENS)
    return jnp.where(quick_heads, quick, slow).astype(jnp.float32)


def draw_queries(key, part):
    shape = (2, TOKENS, Q_HEADS * HEAD)
    base = jax.random.fold_in(key, 1)
    values = jax.random.truncated_normal(base, -6.0, 6.0, shape)
    return values.astype(jnp.float32).astype(jnp.bfloat16)


def draw_keys_values(key, part):
    shape = (2, TOKENS, KV_HEADS * HEAD)
    base = jax.random.fold_in(key, 2)
    values = jax.random.truncated_normal(base, -6.0, 6.0, shape)
    return values.astype(jnp.float32).astype(jnp.bfloat16)


def steps_of(own_key, shape, pieces, smallest, top_value):
    level, own = 1.0, jax.random.fold_in(own_key, 6)
    for position, shards_of in pieces:
        steps = jnp.exp(jax.random.uniform(jax.random.fold_in(own, position), (shards_of,), jnp.float32, smallest / len(pieces), top_value / len(pieces)))
        level = level * jnp.repeat(steps, shape[position] // shards_of).reshape([-1 if axis == position else 1 for axis in range(len(shape))])
    return level


def length_profile(amount, total, most, slope):
    portions = [(1 << 20) // math.isqrt(standing ** slope) + 1 for standing in range(2, amount + 1)]
    spare, holding = total - most - (amount - 1), [1] * (amount - 1)
    while spare > 0:
        candidates = [i for i in range(amount - 1) if holding[i] < most]
        whole, remaining = sum([portions[i] for i in candidates]), spare
        for i in candidates:
            addition = min(most - holding[i], max(1, remaining * portions[i] // whole), spare)
            holding[i] = holding[i] + addition
            spare = spare - addition
    return np.array([most] + holding)


def ragged(stream_key, number_of, total, limit, lean):
    if number_of == 2:
        one = jax.random.randint(stream_key, (), max(1, total - limit), min(limit, total - 1) + 1)
        return jnp.stack([one, total - one])
    tallies = jnp.asarray(length_profile(number_of, total, limit, lean), jnp.int32)
    twos = (number_of - 1) // 2
    giver, receiver = tallies[1:1 + 2 * twos:2], tallies[2:2 + 2 * twos:2]
    margin = jnp.minimum(giver - 1, limit - receiver)
    shifted = jax.random.randint(jax.random.fold_in(stream_key, 1), (twos,), 0, 1 << 20) % (margin + 1)
    tallies = tallies.at[1:1 + 2 * twos:2].set(giver - shifted).at[2:2 + 2 * twos:2].set(receiver + shifted)
    return tallies[jax.random.permutation(jax.random.fold_in(stream_key, 2), number_of)]


def noise(stream_key, shape, spread, limit, cuts=(), kind=jnp.bfloat16):
    gain = steps_of(stream_key, shape, cuts, -0.22, 0.18) if cuts else 1.0
    entries = jax.random.normal(stream_key, shape, jnp.float32) * spread * gain
    return jnp.minimum(jnp.maximum(entries, -limit), limit).astype(kind)


def setup_inputs(seed: int = 0, part: int = 0) -> dict:
    arg_keys = jax.random.split(jax.random.key(seed), 9)
    part_keys = jax.random.split(jax.random.fold_in(arg_keys[8], part), 9)
    ssm_inputs = noise(part_keys[0], (TOKENS, HEADS_SSM * HEAD_SSM), 1.0, 6.0, ((0, 16),))
    state_write = noise(part_keys[1], (TOKENS, STATE), 1.0, 6.0, ((0, 16),))
    state_read = noise(part_keys[2], (TOKENS, STATE), 1.0, 6.0, ((0, 16),))
    decay_codes = draw_decay_codes(jax.random.fold_in(jax.random.fold_in(arg_keys[8], part), 71), part)
    decay_rate = draw_decay_rate(jax.random.fold_in(arg_keys[8], 71), part)
    queries = draw_queries(jax.random.fold_in(jax.random.fold_in(arg_keys[8], part), 71), part)
    keys_values = draw_keys_values(jax.random.fold_in(jax.random.fold_in(arg_keys[8], part), 71), part)
    segment_ids = jnp.searchsorted(jnp.cumsum(ragged(part_keys[7], 4, TOKENS, TOKENS // 2, 0)), jnp.arange(TOKENS), side="right").astype(jnp.int32)
    return {"ssm_inputs": ssm_inputs, "state_write": state_write, "state_read": state_read, "decay_codes": decay_codes, "decay_rate": decay_rate, "queries": queries, "keys_values": keys_values, "segment_ids": segment_ids}


def log_decay(codes, rates):
    lower = (codes % 1024).astype(jnp.float32)
    level = (codes // 1024).astype(jnp.float32)
    return -rates[None, :] * (1.0 + lower / 128.0) - 0.125 * level

def ssm_block(state, block):
    inputs, write_map, read_map, steps_log = block
    length = inputs.shape[0]
    running = jnp.cumsum(steps_log, axis=0)
    trailing = running.T
    spread_log = trailing[:, :, None] - trailing[:, None, :]
    causal_pairs = lax.broadcasted_iota(jnp.int32, (length, length), 0) >= lax.broadcasted_iota(jnp.int32, (length, length), 1)
    damping = jnp.where(causal_pairs[None], jnp.exp(jnp.minimum(spread_log, 0.0)), 0.0)
    inner_products = jnp.dot(read_map, write_map.T, preferred_element_type=jnp.float32)
    mixing = (inner_products[None] * damping).astype(jnp.bfloat16)
    mixing = lax.optimization_barrier(mixing)
    local_part = jnp.einsum('hts,shp->thp', mixing.astype(jnp.float32), inputs.astype(jnp.float32), precision=lax.Precision.HIGHEST)
    to_block_end = jnp.exp(running[-1][None, :] - running)
    scaled = (to_block_end[:, :, None] * inputs.astype(jnp.float32)).astype(jnp.bfloat16)
    scaled = lax.optimization_barrier(scaled)
    contribution = jnp.einsum('shp,sn->hpn', scaled.astype(jnp.float32), write_map.astype(jnp.float32), precision=lax.Precision.HIGHEST)
    carried = jnp.einsum('tn,hpn->thp', read_map.astype(jnp.float32), state, precision=lax.Precision.HIGHEST)
    carried = carried * jnp.exp(running)[:, :, None]
    next_state = jnp.exp(running[-1])[:, None, None] * state + contribution
    return (next_state, local_part + carried)

def attend_layer(layer_queries, keys, values, segments):
    group_size = Q_HEADS // KV_HEADS
    block_rows = min(512, TOKENS)
    span = WINDOW + block_rows
    keys_padded = jnp.pad(keys.reshape(TOKENS, KV_HEADS, HEAD).astype(jnp.float32), ((WINDOW, 0), (0, 0), (0, 0)))
    values_padded = jnp.pad(values.reshape(TOKENS, KV_HEADS, HEAD).astype(jnp.float32), ((WINDOW, 0), (0, 0), (0, 0)))
    segments_padded = jnp.pad(segments, (WINDOW, 0), constant_values=-1)

    def one_block(block_index):
        first_row = (block_index * block_rows).astype(jnp.int32)
        block_queries = lax.dynamic_slice_in_dim(layer_queries, first_row, block_rows, 0)
        block_queries = block_queries.reshape(block_rows, KV_HEADS, group_size, HEAD).astype(jnp.float32)
        query_pos = first_row + jnp.arange(block_rows, dtype=jnp.int32)
        query_segments = lax.dynamic_slice_in_dim(segments, first_row, block_rows, 0)
        block_keys = lax.dynamic_slice_in_dim(keys_padded, first_row, span, 0)
        block_values = lax.dynamic_slice_in_dim(values_padded, first_row, span, 0)
        key_segments = lax.dynamic_slice_in_dim(segments_padded, first_row, span, 0)
        key_pos = first_row - WINDOW + jnp.arange(span, dtype=jnp.int32)
        scores = jnp.einsum('qgrd,kgd->grqk', block_queries, block_keys, precision=lax.Precision.HIGHEST) * HEAD ** (-0.5)
        allowed = (key_pos[None, :] <= query_pos[:, None]) & (key_pos[None, :] > query_pos[:, None] - WINDOW)
        allowed = allowed & (key_pos[None, :] >= 0) & (key_segments[None, :] == query_segments[:, None])
        masked = jnp.where(allowed, scores, -1e+30)
        peak = lax.optimization_barrier(jnp.max(masked, axis=-1, keepdims=True))
        probs = jnp.where(allowed, jnp.exp(masked - peak), 0.0)
        totals = lax.optimization_barrier(jnp.sum(probs, axis=-1))
        weights = lax.optimization_barrier(probs.astype(jnp.bfloat16))
        weighted = jnp.einsum('grqk,kgd->qgrd', weights.astype(jnp.float32), block_values, precision=lax.Precision.HIGHEST)
        result = weighted / jnp.transpose(totals, (2, 0, 1))[..., None]
        return result.reshape(block_rows, Q_HEADS * HEAD)
    blocks = lax.map(one_block, jnp.arange(TOKENS // block_rows, dtype=jnp.int32))
    return blocks.reshape(TOKENS, Q_HEADS * HEAD)

def reference(ssm_inputs, state_write, state_read, decay_codes, decay_rate, queries, keys_values, segment_ids):
    steps_log = log_decay(decay_codes, decay_rate)
    blocks = (ssm_inputs.reshape(N_SEQ, TOK_DEV, HEADS_SSM, HEAD_SSM), state_write.reshape(N_SEQ, TOK_DEV, STATE), state_read.reshape(N_SEQ, TOK_DEV, STATE), steps_log.reshape(N_SEQ, TOK_DEV, HEADS_SSM))
    start_state = jnp.zeros((HEADS_SSM, HEAD_SSM, STATE), jnp.float32)
    _, mixed = lax.scan(ssm_block, start_state, blocks)
    mixed = mixed.reshape(TOKENS, HEADS_SSM, HEAD_SSM)
    mean_square = lax.optimization_barrier(jnp.mean(mixed * mixed, axis=-1, keepdims=True))
    ssm_output = (mixed * lax.rsqrt(mean_square + 1e-05)).reshape(TOKENS, HEADS_SSM * HEAD_SSM).astype(jnp.bfloat16)
    layers = [attend_layer(queries[layer], keys_values[0], keys_values[1], segment_ids) for layer in range(2)]
    attn_output = jnp.stack(layers).astype(jnp.bfloat16)
    return (ssm_output, attn_output)
```

```python
import functools
import math

import jax
import jax.numpy as jnp
from jax import lax
from jax.experimental import pallas as pl
from jax.experimental.pallas import tpu as pltpu
from jax.sharding import PartitionSpec as P

KV_HEADS = 4
HEAD = 128
WINDOW = 1024
ROW = 4
FAR = -1e30
SCALE = HEAD ** (-0.5) * math.log2(math.e)
F32 = jnp.float32
BF16 = jnp.bfloat16
VMEM = pltpu.VMEM


def nt_dot(a, b):
    return lax.dot_general(a, b, (((1,), (1,)), ((), ())), preferred_element_type=F32)


def tn_dot(a, b, precision=None):
    return lax.dot_general(
        a, b, (((0,), (0,)), ((), ())), preferred_element_type=F32, precision=precision
    )


def call(kernel, name, outs, flops, moved, trans, **rest):
    return pl.pallas_call(
        kernel,
        name=name,
        out_shape=outs,
        cost_estimate=pl.CostEstimate(
            flops=int(flops), bytes_accessed=int(moved), transcendentals=int(trans)
        ),
        compiler_params=pltpu.CompilerParams(vmem_limit_bytes=48 * 1024 * 1024),
        **rest,
    )


def attend_kernel(kinds, first, last, tokens, *refs):
    count = len(kinds)
    q_ref, seg_ref = refs[0], refs[1]
    pieces = refs[2 : 2 + count]
    at = 2 + count
    if not first:
        acc_in, stat_in = refs[at : at + 2]
        at += 2
    if last:
        out_ref = refs[at]
        at += 1
    else:
        acc_out, stat_out = refs[at : at + 2]
        at += 2
    k_all, v_all, bias = refs[at : at + 3]
    head = pl.program_id(0)
    rows = tokens

    @pl.when(head == 0)
    def _():
        mine = seg_ref[...]
        i = lax.broadcasted_iota(jnp.int32, (rows, rows), 0)
        j = lax.broadcasted_iota(jnp.int32, (rows, rows), 1)
        for n, kind in enumerate(kinds):
            theirs = pieces[n][2 * rows : 2 * rows + 1, 0:rows].astype(F32)
            same = theirs == mine
            if kind == "own":
                same = same & (j <= i)
            if kind == "edge":
                same = same & (j > i)
            bias[:, n * rows : (n + 1) * rows] = jnp.where(same, 0.0, FAR)
        v_all[:, HEAD:] = jnp.ones((count * rows, HEAD), BF16)

    lanes = pl.ds(pl.multiple_of(head * HEAD, HEAD), HEAD)
    for n in range(count):
        k_all[n * rows : (n + 1) * rows, :] = pieces[n][0:rows, lanes]
        v_all[n * rows : (n + 1) * rows, 0:HEAD] = pieces[n][rows : 2 * rows, lanes]
    keys = k_all[...]
    values = v_all[...]
    group = q_ref.shape[2] // HEAD
    for layer in range(2):
        for r in range(group):
            slot = layer * group + r
            cols = slice(r * HEAD, (r + 1) * HEAD)
            scores = nt_dot(q_ref[layer, :, cols], keys) * SCALE + bias[...]
            peak = jnp.max(scores, axis=1, keepdims=True)
            if not first:
                old_peak = stat_in[0, :, slot : slot + 1]
                peak = jnp.maximum(peak, old_peak)
            probs = jnp.exp2(scores - peak)
            both = jnp.dot(probs.astype(BF16), values, preferred_element_type=F32)
            total = both[:, HEAD:]
            acc = both[:, :HEAD]
            if not first:
                fade = jnp.exp2(old_peak - peak)
                acc = acc + fade * acc_in[layer, :, cols]
                total = total + fade * stat_in[0, :, 8 + slot : 9 + slot]
            if last:
                out_ref[layer, :, cols] = (acc / total).astype(BF16)
            else:
                acc_out[layer, :, cols] = acc
                stat_out[0, :, slot : slot + 1] = peak
                stat_out[0, :, 8 + slot : 9 + slot] = total[:, 0:1]


def attend(queries, segs, pieces, kinds, carry, last):
    layers, tokens, width = queries.shape
    block = width // KV_HEADS
    count = len(kinds)
    wide = pl.BlockSpec((layers, tokens, block), lambda h: (0, 0, h))
    stat = pl.BlockSpec((1, tokens, HEAD), lambda h: (h, 0, 0))
    whole = lambda x: pl.BlockSpec(x.shape, lambda h: (0,) * x.ndim)
    in_specs = [wide, whole(segs)] + [whole(p) for p in pieces]
    args = [queries, segs] + list(pieces)
    if carry is not None:
        in_specs += [wide, stat]
        args += list(carry)
    if last:
        outs = jax.ShapeDtypeStruct(queries.shape, BF16)
        out_specs = wide
    else:
        outs = (
            jax.ShapeDtypeStruct(queries.shape, F32),
            jax.ShapeDtypeStruct((KV_HEADS, tokens, HEAD), F32),
        )
        out_specs = (wide, stat)
    work = layers * tokens * width * tokens * count
    return call(
        functools.partial(attend_kernel, kinds, carry is None, last, tokens),
        "attend",
        outs,
        4 * work,
        4 * queries.size * 2,
        work // HEAD,
        grid=(KV_HEADS,),
        in_specs=in_specs,
        out_specs=out_specs,
        scratch_shapes=[
            VMEM((count * tokens, HEAD), BF16),
            VMEM((count * tokens, 2 * HEAD), BF16),
            VMEM((tokens, count * tokens), F32),
        ],
    )(*args)


def spread(columns, first, pairs, width):
    lane = lax.broadcasted_iota(jnp.int32, (1, 2 * width), 1)
    parts = [
        jnp.where(
            lane < width,
            columns[:, first + 2 * k : first + 2 * k + 1],
            columns[:, first + 2 * k + 1 : first + 2 * k + 2],
        )
        for k in range(pairs)
    ]
    return jnp.concatenate(parts, axis=1)


def local_kernel(
    heads, state, place, x_ref, own_ref, y_ref, c_ref, rate_ref, mixed_ref, tail_ref, run_ref,
    read_ref, xs, sm
):
    tokens = x_ref.shape[0]
    cols = xs.shape[2]
    width = cols // heads
    q = place[0]
    core = lax.rem(q, 2)
    lanes = lambda n: pl.ds(pl.multiple_of(n * cols, cols), cols)
    xs[q] = x_ref[:, lanes(q)]
    sm[q] = own_ref[...]
    xs[q ^ 2] = y_ref[:, lanes(core)]
    sm[q ^ 2] = y_ref[:, 2 * cols :]
    xs[q ^ 1] = c_ref[0:tokens, 0:cols]
    sm[q ^ 1] = c_ref[0:tokens, cols:]
    xs[q ^ 3] = c_ref[tokens:, 0:cols]
    sm[q ^ 3] = c_ref[tokens:, cols:]

    i = lax.broadcasted_iota(jnp.int32, (tokens, tokens), 0)
    j = lax.broadcasted_iota(jnp.int32, (tokens, tokens), 1)
    causal = j <= i
    lower_ones = causal.astype(F32)
    upper_ones = (i <= j).astype(F32)
    lane = lax.broadcasted_iota(jnp.int32, (1, 2 * width), 1)
    low = lane < width
    rates = rate_ref[0:1, :]
    shift = lax.rem(128 - q * heads, 128)
    carried_state = jnp.zeros((state, cols), F32)
    offset = jnp.zeros((1, 128), F32)
    for b in range(ROW):
        write = sm[b, :, 0:state]
        read = sm[b, :, state : 2 * state]
        read_ref[b] = read
        codes = sm[b, :, 2 * state :].astype(F32)
        high = codes
        little = pltpu.roll(codes, 64, 1)
        level = jnp.floor(high * 0.0625)
        lower = high * 64.0 + little - 1024.0 * level
        step = -rates * (1.0 + lower * (1.0 / 128.0)) - 0.125 * level
        step = pltpu.roll(step, shift, 1)
        step = jnp.where(j < heads, step, 0.0)
        run = jnp.dot(
            lower_ones, step, preferred_element_type=F32, precision=lax.Precision.HIGHEST
        )
        run_t = tn_dot(step, upper_ones, lax.Precision.HIGHEST)
        end = run[tokens - 1 : tokens, :]
        run_ref[b] = run + offset
        offset = offset + end
        inner = nt_dot(read, write)
        inner = jnp.where(causal, inner, 0.0)
        to_end = jnp.exp(end - run)
        locals_ = []
        scaled = []
        for pair in range(heads // 2):
            tile = xs[b, :, pair * 2 * width : (pair + 1) * 2 * width]
            mixes = []
            for h in (2 * pair, 2 * pair + 1):
                gap = jnp.minimum(run[:, h : h + 1] - run_t[h : h + 1, :], 0.0)
                mixes.append((inner * jnp.exp(gap)).astype(BF16))
            zero = jnp.zeros_like(tile)
            stacked = jnp.concatenate(
                [jnp.where(low, tile, zero), jnp.where(low, zero, tile)], axis=0
            )
            locals_.append(
                jnp.dot(jnp.concatenate(mixes, axis=1), stacked, preferred_element_type=F32)
            )
            weight = jnp.where(
                low, to_end[:, 2 * pair : 2 * pair + 1], to_end[:, 2 * pair + 1 : 2 * pair + 2]
            )
            scaled.append((weight * tile.astype(F32)).astype(BF16))
        mixed = jnp.concatenate(locals_, axis=1)
        if b > 0:
            seen = jnp.dot(read, carried_state.astype(BF16), preferred_element_type=F32)
            mixed = mixed + spread(jnp.exp(run), 0, heads // 2, width) * seen
        mixed_ref[b] = mixed
        added = tn_dot(write, jnp.concatenate(scaled, axis=1))
        if b > 0:
            added = spread(jnp.exp(end), 0, heads // 2, width) * carried_state + added
        carried_state = added
    tail_ref[0:state, :] = carried_state.astype(BF16)
    log_total = spread(offset, 0, heads // 2, width)
    one = log_total.astype(BF16)
    rest = log_total - one.astype(F32)
    two = rest.astype(BF16)
    three = (rest - two.astype(F32)).astype(BF16)
    row = lax.broadcasted_iota(jnp.int32, (16, cols), 0)
    tail_ref[state:, :] = jnp.where(row == 0, one, jnp.where(row == 1, two, three))


def finish_kernel(
    heads, state, rows, place, mixed_ref, tails_ref, run_ref, read_ref, self_ref, c_ref, y_ref
):
    q = place[0]
    z = place[1]
    cols = mixed_ref.shape[2]
    width = cols // heads
    entering = jnp.zeros((state, cols), F32)
    for n in range(rows - 1):
        logs = tails_ref[n, state:, :].astype(F32)
        decay = jnp.exp(logs[0:1] + logs[1:2] + logs[2:3])
        later = decay * entering + tails_ref[n, 0:state, :].astype(F32)
        entering = jnp.where(n < z, later, entering)
    entering = entering.astype(BF16)
    a = lax.broadcasted_iota(jnp.int32, (4 * width, 2 * width), 0)
    b = lax.broadcasted_iota(jnp.int32, (4 * width, 2 * width), 1)
    same = (lax.rem(a, 2 * width) < width) == (b < width)
    average = jnp.where(same, 1.0 / width, 0.0).astype(BF16)
    for near in range(ROW):
        at = q ^ near
        seen = jnp.dot(read_ref[at], entering, preferred_element_type=F32)
        fade = spread(jnp.exp(run_ref[at]), 0, heads // 2, width)
        mixed = mixed_ref[at] + fade * seen
        for pair in range(heads // 2):
            part = slice(pair * 2 * width, (pair + 1) * 2 * width)
            tile = mixed[:, part]
            square = tile * tile
            big = square.astype(BF16)
            small = (square - big.astype(F32)).astype(BF16)
            mean = jnp.dot(
                jnp.concatenate([big, small], axis=1), average, preferred_element_type=F32
            )
            result = (tile * lax.rsqrt(mean + 1e-05)).astype(BF16)
            if near == 0:
                self_ref[:, part] = result
            elif near == 1:
                c_ref[:, part] = result
            else:
                y_ref[near - 2, :, part] = result


def gather_kernel(place, self_ref, y_ref, c_ref, out_ref):
    q = place[0]
    cols = self_ref.shape[1]
    lanes = lambda n: pl.ds(pl.multiple_of(n * cols, cols), cols)
    out_ref[:, lanes(q)] = self_ref[...]
    out_ref[:, lanes(q ^ 2)] = y_ref[0]
    out_ref[:, lanes(q ^ 1)] = c_ref[0]
    out_ref[:, lanes(q ^ 3)] = c_ref[1]


def shards(
    ssm_inputs, state_write, state_read, decay_codes, decay_rate, queries, keys_values, segment_ids
):
    tokens, channels = ssm_inputs.shape
    heads = decay_rate.shape[0]
    state = state_write.shape[1]
    own_heads = heads // ROW
    cols = channels // ROW
    devices = lax.axis_size("seq")
    rows = devices // ROW
    rank = lax.axis_index("seq")
    q = rank % ROW
    core, y = q % 2, q // 2
    place = jnp.stack([q, rank // ROW]).astype(jnp.int32)
    swap_c = [(i, i ^ 1) for i in range(devices)]
    swap_y = [(i, i ^ 2) for i in range(devices)]
    up_z = [(i, i + ROW) for i in range(devices - ROW)]
    c_up = [(i, i + 1) for i in range(0, devices, 2)]
    c_down = [(i + 1, i) for i in range(0, devices, 2)]
    send = lambda x, route: lax.ppermute(x, "seq", route)
    smem = pl.BlockSpec(memory_space=pltpu.SMEM)
    vmem = pl.BlockSpec(memory_space=pltpu.VMEM)

    seg_codes = (segment_ids + 1).astype(BF16)
    kv_width = keys_values.shape[2]
    seg_rows = jnp.broadcast_to(
        jnp.pad(seg_codes, (0, kv_width - tokens))[None, :], (16, kv_width)
    )
    own = jnp.concatenate([keys_values[0], keys_values[1], seg_rows], axis=0)
    segs = jnp.broadcast_to(seg_codes.astype(F32)[:, None], (tokens, tokens))

    codes = jnp.concatenate(
        [
            jnp.pad((decay_codes // 64).astype(BF16), ((0, 0), (0, 64 - heads))),
            jnp.pad((decay_codes % 64).astype(BF16), ((0, 0), (0, 64 - heads))),
        ],
        axis=1,
    )
    small = jnp.concatenate([state_write, state_read, codes], axis=1)
    to_y = jnp.concatenate(
        [lax.dynamic_slice_in_dim(ssm_inputs, (1 - y) * 2 * cols, 2 * cols, 1), small], axis=1
    )
    from_y = send(to_y, swap_y)
    behind2 = send(own, up_z)
    partner = send(own, c_up)
    to_c = jnp.concatenate(
        [
            jnp.concatenate(
                [lax.dynamic_slice_in_dim(ssm_inputs, (q ^ 1) * cols, cols, 1), small], axis=1
            ),
            jnp.concatenate(
                [
                    lax.dynamic_slice_in_dim(from_y, (1 - core) * cols, cols, 1),
                    from_y[:, 2 * cols :],
                ],
                axis=1,
            ),
        ],
        axis=0,
    )
    from_c = send(to_c, swap_c)

    carry = attend(queries, segs, [own, partner], ("own", "any"), None, False)

    rates = jnp.broadcast_to(jnp.pad(decay_rate, (0, 128 - heads))[None, :], (8, 128))
    mixed, tail, run, reads = call(
        functools.partial(local_kernel, own_heads, state),
        "local",
        (
            jax.ShapeDtypeStruct((ROW, tokens, cols), F32),
            jax.ShapeDtypeStruct((state + 16, cols), BF16),
            jax.ShapeDtypeStruct((ROW, tokens, 128), F32),
            jax.ShapeDtypeStruct((ROW, tokens, state), BF16),
        ),
        ROW * tokens * cols * tokens * 8,
        4 * 1024 * 1024,
        ROW * own_heads * tokens * tokens,
        in_specs=[smem] + [vmem] * 5,
        out_specs=(vmem,) * 4,
        scratch_shapes=[
            VMEM((ROW, tokens, cols), BF16),
            VMEM((ROW, tokens, 2 * state + 128), BF16),
        ],
    )(place, ssm_inputs, small, from_y, from_c, rates)
    groups = [[i + ROW * n for n in range(rows)] for i in range(ROW)]
    tails = lax.all_gather(tail, "seq", axis_index_groups=groups)

    behind1 = send(jnp.where(y == 0, own, behind2), swap_y)
    behind4 = send(behind2, up_z)
    behind2c = send(behind2, swap_c)
    behind1c = send(behind1, swap_c)
    carry = attend(
        queries, segs, [behind2, behind2c, behind1, behind1c], ("any",) * 4, carry, False
    )
    behind3 = send(jnp.where(y == 0, behind2, behind4), swap_y)
    behind4c = send(behind4, c_down)
    behind3c = send(behind3, swap_c)

    mine, for_c, for_y = call(
        functools.partial(finish_kernel, own_heads, state, rows),
        "finish",
        (
            jax.ShapeDtypeStruct((tokens, cols), BF16),
            jax.ShapeDtypeStruct((tokens, cols), BF16),
            jax.ShapeDtypeStruct((2, tokens, cols), BF16),
        ),
        ROW * tokens * cols * tokens * 6,
        4 * 1024 * 1024,
        ROW * tokens * cols,
        in_specs=[smem] + [vmem] * 4,
        out_specs=(vmem,) * 3,
    )(place, mixed, tails, run, reads)
    back_y = send(for_y, swap_y)
    back_c = send(jnp.stack([for_c, back_y[1]]), swap_c)

    attn_output = attend(
        queries, segs, [behind4, behind4c, behind3, behind3c], ("edge",) + ("any",) * 3, carry, True
    )
    ssm_output = call(
        gather_kernel,
        "collect",
        jax.ShapeDtypeStruct((tokens, channels), BF16),
        0,
        1024 * 1024,
        0,
        in_specs=[smem] + [vmem] * 3,
        out_specs=vmem,
    )(place, mine, back_y, back_c)
    return (ssm_output, attn_output)


def solution(mesh):
    return jax.shard_map(
        shards,
        mesh=mesh,
        in_specs=(
            P(("groups", "seq"), None),
            P(("groups", "seq"), None),
            P(("groups", "seq"), None),
            P(("groups", "seq"), None),
            P(),
            P(None, ("groups", "seq"), None),
            P(None, ("groups", "seq"), None),
            P(("groups", "seq")),
        ),
        out_specs=(P(("groups", "seq"), None), P(None, ("groups", "seq"), None)),
        check_vma=False,
    )
```

```python
import functools
import math

import jax
import jax.numpy as jnp
from jax import lax
from jax.experimental import pallas as pl
from jax.experimental.pallas import tpu as pltpu
from jax.sharding import PartitionSpec as P

KV_HEADS = 4
HEAD = 128
ROW = 4
FAR = -1e30
SCALE = HEAD ** (-0.5) * math.log2(math.e)
F32 = jnp.float32
BF16 = jnp.bfloat16
VMEM = pltpu.VMEM
IN_SMEM = pl.BlockSpec(memory_space=pltpu.SMEM)
IN_VMEM = pl.BlockSpec(memory_space=pltpu.VMEM)
LOGS = 16


def nt_dot(a, b):
    return lax.dot_general(a, b, (((1,), (1,)), ((), ())), preferred_element_type=F32)


def tn_dot(a, b, precision=None):
    return lax.dot_general(
        a, b, (((0,), (0,)), ((), ())), preferred_element_type=F32, precision=precision
    )


def lanes(number, width):
    return pl.ds(pl.multiple_of(number * width, width), width)


def call(kernel, name, micros, place, args, outs, scratch=()):
    return pl.pallas_call(
        kernel,
        name=name,
        out_shape=outs,
        in_specs=[IN_SMEM] + [IN_VMEM] * len(args),
        out_specs=jax.tree.map(lambda _: IN_VMEM, outs),
        scratch_shapes=list(scratch),
        cost_estimate=pl.CostEstimate(
            flops=int(micros * 1.15e9), bytes_accessed=0, transcendentals=0
        ),
        compiler_params=pltpu.CompilerParams(vmem_limit_bytes=24 * 1024 * 1024),
    )(place, *args)


def shaped(*shape, dtype=BF16):
    return jax.ShapeDtypeStruct(shape, dtype)


def pack_kernel(place, x_ref, write_ref, read_ref, codes_ref, kv_ref, seg_ref, own, small, to_c):
    core = place[0]
    tokens, state = write_ref.shape
    heads = codes_ref.shape[1]
    own[0:tokens, :] = kv_ref[0]
    own[tokens : 2 * tokens, :] = kv_ref[1]
    seg = (seg_ref[...] + 1).astype(F32).astype(BF16)
    own[2 * tokens :, 0:tokens] = jnp.broadcast_to(seg, (16, tokens))
    own[2 * tokens :, tokens:] = jnp.zeros((16, own.shape[1] - tokens), BF16)
    codes = codes_ref[...]
    high = (codes >> 6).astype(F32)
    low = (codes & 63).astype(F32)
    gap = jnp.zeros((tokens, 64 - heads), F32)
    both = jnp.concatenate([high, gap, low, gap], axis=1).astype(BF16)
    small[:, 0:state] = write_ref[...]
    small[:, state : 2 * state] = read_ref[...]
    small[:, 2 * state :] = both
    half = x_ref.shape[1] // 2
    to_c[:, 0:half] = x_ref[:, lanes(1 - core, half)]
    to_c[:, half : half + state] = write_ref[...]
    to_c[:, half + state : half + 2 * state] = read_ref[...]
    to_c[:, half + 2 * state :] = both


def attend_kernel(kinds, first, last, place, q_ref, own_ref, *refs):
    count = len(kinds)
    rows = q_ref.shape[1]
    pieces = refs[:count]
    at = count
    if not first:
        acc_in, peak_in, sum_in = refs[at : at + 3]
        at += 3
    if last:
        out_ref = refs[at]
        at += 1
    else:
        acc_out, peak_out, sum_out = refs[at : at + 3]
        at += 3
    k_all, v_all, bias = refs[at : at + 3]
    core = place[0]
    chip = place[3]
    codes = own_ref[2 * rows : 2 * rows + 16, 0:rows].astype(F32)
    mine = jnp.transpose(jnp.broadcast_to(codes[0:1], (rows, rows)))
    i = lax.broadcasted_iota(jnp.int32, (rows, rows), 0)
    j = lax.broadcasted_iota(jnp.int32, (rows, rows), 1)
    for n, (behind, other) in enumerate(kinds):
        theirs = pieces[n][2 * rows : 2 * rows + 16, 0:rows].astype(F32)[0:1]
        if behind == 0 and not other:
            ok = j <= i
        elif behind == 0:
            ok = j < rows * core
        elif behind == 4 and not other:
            ok = j > i + jnp.where(chip >= behind, 0, rows)
        elif behind == 4:
            ok = j < jnp.where((chip >= behind) & (core == 0), rows, 0)
        else:
            ok = j < jnp.where(chip >= behind, rows, 0)
        bias[:, n * rows : (n + 1) * rows] = jnp.where((theirs == mine) & ok, 0.0, FAR)
    v_all[:, HEAD:] = jnp.ones((count * rows, HEAD), BF16)
    group = q_ref.shape[2] // HEAD // KV_HEADS

    def one(head, _):
        here = lanes(head, HEAD)
        for n in range(count):
            k_all[n * rows : (n + 1) * rows, :] = pieces[n][0:rows, here]
            v_all[n * rows : (n + 1) * rows, 0:HEAD] = pieces[n][rows : 2 * rows, here]
        for layer in range(2):
            for r in range(group):
                cols = lanes(head * group + r, HEAD)
                scores = nt_dot(q_ref[layer, :, cols], k_all[...]) * SCALE + bias[...]
                peak = jnp.max(scores, axis=1, keepdims=True)
                if first:
                    probs = jnp.exp2(scores - peak)
                else:
                    old = peak_in[layer, :, cols]
                    peak = jnp.maximum(old, peak)
                    fade = jnp.exp2(old - peak)
                    probs = jnp.concatenate(
                        [
                            jnp.exp2(scores[:, n * rows : (n + 1) * rows] - peak)
                            for n in range(count)
                        ],
                        axis=1,
                    )
                both = jnp.dot(probs.astype(BF16), v_all[...], preferred_element_type=F32)
                acc = both[:, :HEAD]
                total = both[:, HEAD:]
                if not first:
                    acc = acc + fade * acc_in[layer, :, cols]
                    total = total + fade * sum_in[layer, :, cols]
                if last:
                    out_ref[layer, :, cols] = (acc / total).astype(BF16)
                else:
                    acc_out[layer, :, cols] = acc
                    sum_out[layer, :, cols] = total
                    peak_out[layer, :, cols] = jnp.broadcast_to(peak, (rows, HEAD))
        return _

    lax.fori_loop(0, KV_HEADS, one, 0)


def attend(place, queries, own, pieces, kinds, carry, last):
    layers, tokens, width = queries.shape
    count = len(kinds)
    partial = shaped(layers, tokens, width, dtype=F32)
    return call(
        functools.partial(attend_kernel, kinds, carry is None, last),
        "attend%d" % kinds[-1][0],
        0.5 + 1.05 * count,
        place,
        [queries, own] + list(pieces) + list(carry or ()),
        shaped(layers, tokens, width) if last else (partial,) * 3,
        [
            VMEM((count * tokens, HEAD), BF16),
            VMEM((count * tokens, 2 * HEAD), BF16),
            VMEM((tokens, count * tokens), F32),
        ],
    )


def spread(columns, pairs, width):
    low = lax.broadcasted_iota(jnp.int32, (1, 2 * width), 1) < width
    parts = [
        jnp.where(low, columns[:, 2 * k : 2 * k + 1], columns[:, 2 * k + 1 : 2 * k + 2])
        for k in range(pairs)
    ]
    return jnp.concatenate(parts, axis=1)


def put_logs(ref, state, logs):
    one = logs.astype(BF16)
    rest = logs - one.astype(F32)
    two = rest.astype(BF16)
    three = (rest - two.astype(F32)).astype(BF16)
    row = lax.broadcasted_iota(jnp.int32, (LOGS, logs.shape[1]), 0)
    ref[state:, :] = jnp.where(row == 0, one, jnp.where(row == 1, two, three))


def get_logs(ref, state, cols):
    parts = ref[state:, cols].astype(F32)
    return parts[0:1] + parts[1:2] + parts[2:3]


def local_kernel(
    heads, state, place, x_ref, own_ref, c_ref, rate_ref, mixed_ref, tail_ref, run_ref, read_ref,
    xs, sm
):
    tokens = x_ref.shape[0]
    cols = xs.shape[2]
    width = cols // heads
    core = place[0]
    xs[core] = x_ref[:, lanes(core, cols)]
    sm[core] = own_ref[...]
    xs[1 - core] = c_ref[:, 0:cols]
    sm[1 - core] = c_ref[:, cols:]
    i = lax.broadcasted_iota(jnp.int32, (tokens, tokens), 0)
    j = lax.broadcasted_iota(jnp.int32, (tokens, tokens), 1)
    causal = j <= i
    lower_ones = causal.astype(F32)
    upper_ones = (i <= j).astype(F32)
    low = lax.broadcasted_iota(jnp.int32, (1, 2 * width), 1) < width
    rates = rate_ref[...]
    shift = lax.rem(128 - core * heads, 128)
    kept = None
    offset = None
    for b in range(2):
        write = sm[b, :, 0:state]
        read = sm[b, :, state : 2 * state]
        read_ref[b] = read
        high = sm[b, :, 2 * state :].astype(F32)
        little = pltpu.roll(high, 64, 1)
        level = jnp.floor(high * 0.0625)
        lower = high * 64.0 + little - 1024.0 * level
        step = -rates * (1.0 + lower * (1.0 / 128.0)) - 0.125 * level
        step = jnp.where(j < heads, pltpu.roll(step, shift, 1), 0.0)
        run = jnp.dot(
            lower_ones, step, preferred_element_type=F32, precision=lax.Precision.HIGHEST
        )
        run_t = tn_dot(step, upper_ones, lax.Precision.HIGHEST)
        end = run[tokens - 1 : tokens, :]
        run_ref[b] = run if b == 0 else run + offset
        offset = end if b == 0 else offset + end
        inner = jnp.where(causal, nt_dot(read, write), 0.0)
        to_end = jnp.exp(end - run)
        fade = jnp.exp(run)
        if b > 0:
            seen = jnp.dot(read, kept.astype(BF16), preferred_element_type=F32)
        scaled = []
        for pair in range(heads // 2):
            part = slice(pair * 2 * width, (pair + 1) * 2 * width)
            tile = xs[b, :, part]
            mixes = []
            for h in (2 * pair, 2 * pair + 1):
                gap = jnp.minimum(run[:, h : h + 1] - run_t[h : h + 1, :], 0.0)
                mixes.append((inner * jnp.exp(gap)).astype(BF16))
            zero = jnp.zeros_like(tile)
            stacked = jnp.concatenate(
                [jnp.where(low, tile, zero), jnp.where(low, zero, tile)], axis=0
            )
            mixed = jnp.dot(jnp.concatenate(mixes, axis=1), stacked, preferred_element_type=F32)
            if b > 0:
                mixed = mixed + seen[:, part] * jnp.where(
                    low, fade[:, 2 * pair : 2 * pair + 1], fade[:, 2 * pair + 1 : 2 * pair + 2]
                )
            mixed_ref[b, :, part] = mixed
            weight = jnp.where(
                low, to_end[:, 2 * pair : 2 * pair + 1], to_end[:, 2 * pair + 1 : 2 * pair + 2]
            )
            scaled.append((weight * tile.astype(F32)).astype(BF16))
        added = tn_dot(write, jnp.concatenate(scaled, axis=1))
        if b > 0:
            added = spread(jnp.exp(end), heads // 2, width) * kept + added
        kept = added
    tail_ref[0:state, :] = kept.astype(BF16)
    put_logs(tail_ref, state, spread(offset, heads // 2, width))


def row_kernel(state, place, tail_ref, y_ref, out_ref):
    y = place[1]
    cols = out_ref.shape[1]
    here = lanes(y, cols)
    mine = tail_ref[0:state, here].astype(F32)
    theirs = y_ref[0:state, here].astype(F32)
    my_log = get_logs(tail_ref, state, here)
    their_log = get_logs(y_ref, state, here)
    later = jnp.where(y == 0, theirs, mine)
    earlier = jnp.where(y == 0, mine, theirs)
    decay = jnp.exp(jnp.where(y == 0, their_log, my_log))
    out_ref[0:state, :] = (later + decay * earlier).astype(BF16)
    put_logs(out_ref, state, my_log + their_log)


def hop_kernel(state, distance, last, place, span_ref, before_ref, new_ref, *outs):
    ok = place[2] >= distance
    new = jnp.where(ok, new_ref[0:state, :].astype(F32), 0.0)
    logs = jnp.where(ok, get_logs(new_ref, state, slice(None)), 0.0)
    joined = [(before_ref, outs[0])] if last else [(span_ref, outs[0]), (before_ref, outs[1])]
    for old_ref, out_ref in joined:
        if old_ref is None:
            out_ref[0:state, :] = new.astype(BF16)
            put_logs(out_ref, state, logs)
        else:
            old_logs = get_logs(old_ref, state, slice(None))
            out_ref[0:state, :] = (
                old_ref[0:state, :].astype(F32) + jnp.exp(old_logs) * new
            ).astype(BF16)
            if not last:
                put_logs(out_ref, state, old_logs + logs)


def hop(state, distance, last, place, span, before, new):
    def kernel(place, *refs):
        refs = list(refs)
        span_ref = refs.pop(0)
        before_ref = refs.pop(0) if before is not None else None
        hop_kernel(state, distance, last, place, span_ref, before_ref, *refs)

    out = shaped(state if last else state + LOGS, span.shape[1])
    return call(
        kernel,
        "hop%d" % distance,
        0.6,
        place,
        [span] + ([before] if before is not None else []) + [new],
        (out,) if last else (out, out),
    )


def finish_kernel(
    heads, state, place, mixed_ref, run_ref, read_ref, mine_ref, other_ref, y_ref, self_ref, c_ref
):
    core = place[0]
    y = place[1]
    cols = mixed_ref.shape[2]
    width = cols // heads
    mine = mine_ref[...]
    other = other_ref[...]
    row_in = jnp.concatenate(
        [jnp.where(y == 0, mine, other), jnp.where(y == 0, other, mine)], axis=1
    ).astype(F32)
    decay = jnp.exp(get_logs(y_ref, state, slice(None)))
    entering = jnp.where(y == 0, row_in, y_ref[0:state, :].astype(F32) + decay * row_in)
    entering = entering.astype(BF16)
    a = lax.broadcasted_iota(jnp.int32, (4 * width, 2 * width), 0)
    b = lax.broadcasted_iota(jnp.int32, (4 * width, 2 * width), 1)
    same = (lax.rem(a, 2 * width) < width) == (b < width)
    average = jnp.where(same, 1.0 / width, 0.0).astype(BF16)
    low = lax.broadcasted_iota(jnp.int32, (1, 2 * width), 1) < width
    for out_ref, at in ((c_ref, 1 - core), (self_ref, core)):
        seen = jnp.dot(read_ref[at], entering, preferred_element_type=F32)
        fade = jnp.exp(run_ref[at])
        for pair in range(heads // 2):
            part = slice(pair * 2 * width, (pair + 1) * 2 * width)
            tile = mixed_ref[at, :, part] + seen[:, part] * jnp.where(
                low, fade[:, 2 * pair : 2 * pair + 1], fade[:, 2 * pair + 1 : 2 * pair + 2]
            )
            square = tile * tile
            big = square.astype(BF16)
            small = (square - big.astype(F32)).astype(BF16)
            mean = jnp.dot(
                jnp.concatenate([big, small], axis=1), average, preferred_element_type=F32
            )
            out_ref[:, part] = (tile * lax.rsqrt(mean + 1e-05)).astype(BF16)


def collect_kernel(place, self_ref, c_ref, out_ref):
    core = place[0]
    cols = self_ref.shape[1]
    out_ref[:, lanes(core, cols)] = self_ref[...]
    out_ref[:, lanes(1 - core, cols)] = c_ref[...]


def after(value, *others):
    return lax.optimization_barrier((value, *others))[0]


def shards(
    ssm_inputs, state_write, state_read, decay_codes, decay_rate, queries, keys_values, segment_ids
):
    tokens, channels = ssm_inputs.shape
    heads = decay_rate.shape[0]
    state = state_write.shape[1]
    cols = channels // 2
    devices = lax.axis_size("seq")
    rows = devices // ROW
    rank = lax.axis_index("seq")
    core, y = rank % 2, (rank // 2) % 2
    place = jnp.stack([core, y, rank // ROW, rank // 2]).astype(jnp.int32)
    send = lambda x, route: lax.ppermute(x, "seq", [(i, route(i)) for i in range(devices)])
    swap_c = lambda i: i ^ 1
    swap_y = lambda i: i ^ 2
    up = lambda n: lambda i: (i + n * ROW) % devices
    kv_width = keys_values.shape[2]
    rates = jnp.pad(decay_rate, (0, 128 - heads))[None, :]

    own, small, to_c = call(
        pack_kernel,
        "pack",
        1.5,
        place,
        [ssm_inputs, state_write, state_read, decay_codes, keys_values, segment_ids[None, :]],
        (
            shaped(2 * tokens + 16, kv_width),
            shaped(tokens, 2 * state + 128),
            shaped(tokens, cols + 2 * state + 128),
        ),
    )
    from_c = send(to_c, swap_c)
    behind2 = send(own, up(1))
    partner = send(own, swap_c)

    mixed, tail, run, reads = call(
        functools.partial(local_kernel, heads // 2, state),
        "local",
        4.3,
        place,
        [ssm_inputs, small, from_c, rates],
        (
            shaped(2, tokens, cols, dtype=F32),
            shaped(state + LOGS, cols),
            shaped(2, tokens, 128, dtype=F32),
            shaped(2, tokens, state),
        ),
        [VMEM((2, tokens, cols), BF16), VMEM((2, tokens, 2 * state + 128), BF16)],
    )
    tail_y = send(tail, swap_y)
    behind4 = send(behind2, up(1))
    behind1 = send(jnp.where(y == 0, own, behind2), swap_y)
    behind2c = send(behind2, swap_c)
    carry = attend(
        place,
        after(queries, tail),
        own,
        [own, partner],
        ((0, False), (0, True)),
        None,
        False,
    )

    span = call(
        functools.partial(row_kernel, state),
        "row",
        0.6,
        place,
        [tail, tail_y],
        shaped(state + LOGS, cols // 2),
    )
    before = None
    distance = 1
    while distance < rows:
        new = send(span, up(distance))
        last = 2 * distance >= rows
        out = hop(state, distance, last, place, span, before, new)
        span, before = (None, out[0]) if last else out
        if distance == 1:
            behind3 = send(jnp.where(y == 0, behind2, behind4), swap_y)
            behind1c = send(behind1, swap_c)
            behind4c = send(behind4, swap_c)
            carry = attend(
                place,
                after(queries, carry[0]),
                own,
                [behind2, behind2c, behind1, behind1c],
                ((2, False), (2, True), (1, False), (1, True)),
                carry,
                False,
            )
        distance *= 2
    behind3c = send(behind3, swap_c)
    other_half = send(before, swap_y)
    mine, for_c = call(
        functools.partial(finish_kernel, heads // 2, state),
        "finish",
        1.7,
        place,
        [mixed, run, reads, before, other_half, tail_y],
        (shaped(tokens, cols),) * 2,
    )
    back_c = send(for_c, swap_c)
    attn_output = attend(
        place,
        queries,
        own,
        [behind4, behind4c, behind3, behind3c],
        ((4, False), (4, True), (3, False), (3, True)),
        carry,
        True,
    )
    ssm_output = call(
        collect_kernel, "collect", 0.8, place, [mine, back_c], shaped(tokens, channels)
    )
    return (ssm_output, attn_output)


def solution(mesh):
    return jax.shard_map(
        shards,
        mesh=mesh,
        in_specs=(
            P(("groups", "seq"), None),
            P(("groups", "seq"), None),
            P(("groups", "seq"), None),
            P(("groups", "seq"), None),
            P(),
            P(None, ("groups", "seq"), None),
            P(None, ("groups", "seq"), None),
            P(("groups", "seq")),
        ),
        out_specs=(P(("groups", "seq"), None), P(None, ("groups", "seq"), None)),
        check_vma=False,
    )
```

```python
import functools
import math

import jax
import jax.numpy as jnp
from jax import lax
from jax.experimental import pallas as pl
from jax.experimental.pallas import tpu as pltpu
from jax.sharding import PartitionSpec as P

KV_HEADS = 4
HEAD = 128
ROW = 4
FAR = -1e30
SCALE = HEAD ** (-0.5) * math.log2(math.e)
F32 = jnp.float32
BF16 = jnp.bfloat16
VMEM = pltpu.VMEM
IN_SMEM = pl.BlockSpec(memory_space=pltpu.SMEM)
IN_VMEM = pl.BlockSpec(memory_space=pltpu.VMEM)
LOGS = 16


def nt_dot(a, b):
    return lax.dot_general(a, b, (((1,), (1,)), ((), ())), preferred_element_type=F32)


def tn_dot(a, b, precision=None):
    return lax.dot_general(
        a, b, (((0,), (0,)), ((), ())), preferred_element_type=F32, precision=precision
    )


def lanes(number, width):
    return pl.ds(pl.multiple_of(number * width, width), width)


def call(kernel, name, micros, place, args, outs, scratch=(), stay=False):
    spec = pl.BlockSpec(memory_space=pltpu.HBM) if stay else IN_VMEM
    return pl.pallas_call(
        kernel,
        name=name,
        out_shape=outs,
        in_specs=[IN_SMEM] + [spec] * len(args),
        out_specs=jax.tree.map(lambda _: IN_VMEM, outs),
        scratch_shapes=list(scratch),
        cost_estimate=pl.CostEstimate(
            flops=int(micros * 1.15e9), bytes_accessed=0, transcendentals=0
        ),
        compiler_params=pltpu.CompilerParams(vmem_limit_bytes=24 * 1024 * 1024),
    )(place, *[pltpu.with_memory_space_constraint(a, pltpu.HBM) if stay else a for a in args])


def shaped(*shape, dtype=BF16):
    return jax.ShapeDtypeStruct(shape, dtype)


def pack_kernel(
    place, x, write, read, codes, kv, seg, rate, own, mine, to_c, rates, code_buf, seg_buf, rate_buf,
    sems
):
    core = place[0]
    tokens, state = write.shape
    heads = codes.shape[0]
    half = x.shape[1] // 2
    copies = [
        (kv.at[0], own.at[0:tokens]),
        (kv.at[1], own.at[tokens : 2 * tokens]),
        (x.at[:, lanes(1 - core, half)], to_c.at[:, 0:half]),
        (write, to_c.at[:, half : half + state]),
        (read, to_c.at[:, half + state : half + 2 * state]),
        (codes, code_buf),
        (seg, seg_buf),
        (rate, rate_buf),
        (x.at[:, lanes(core, half)], mine.at[:, 0:half]),
        (write, mine.at[:, half : half + state]),
        (read, mine.at[:, half + state : half + 2 * state]),
    ]
    copies = [
        pltpu.make_async_copy(source, target, sems.at[n])
        for n, (source, target) in enumerate(copies)
    ]
    for copy in copies:
        copy.start()
    own[2 * tokens :, tokens:] = jnp.zeros((16, own.shape[1] - tokens), BF16)
    for copy in copies:
        copy.wait()
    codes_of = (seg_buf[...] + 1).astype(F32).astype(BF16)
    own[2 * tokens :, 0:tokens] = jnp.broadcast_to(codes_of, (16, tokens))
    code = code_buf[...]
    high = (code >> 6).astype(F32)
    low = (code & 63).astype(F32)
    gap = jnp.zeros((64 - heads, tokens), F32)
    both = jnp.transpose(jnp.concatenate([high, gap, low, gap], axis=0)).astype(BF16)
    mine[:, half + 2 * state :] = both
    to_c[:, half + 2 * state :] = both
    rates[...] = jnp.concatenate([rate_buf[...], jnp.zeros((1, 128 - heads), F32)], axis=1)


def attend_kernel(kinds, first, last, place, q_ref, own_ref, *refs):
    count = len(kinds)
    rows = q_ref.shape[1]
    pieces = refs[:count]
    at = count
    if not first:
        acc_in, peak_in, sum_in = refs[at : at + 3]
        at += 3
    if last:
        out_ref = refs[at]
        at += 1
    else:
        acc_out, peak_out, sum_out = refs[at : at + 3]
        at += 3
    k_all, v_all, bias = refs[at : at + 3]
    core = place[0]
    chip = place[3]
    codes = own_ref[2 * rows : 2 * rows + 16, 0:rows].astype(F32)
    mine = jnp.transpose(jnp.broadcast_to(codes[0:1], (rows, rows)))
    i = lax.broadcasted_iota(jnp.int32, (rows, rows), 0)
    j = lax.broadcasted_iota(jnp.int32, (rows, rows), 1)
    for n, (behind, other) in enumerate(kinds):
        theirs = pieces[n][2 * rows : 2 * rows + 16, 0:rows].astype(F32)[0:1]
        if behind == 0 and not other:
            ok = j <= i
        elif behind == 0:
            ok = j < rows * core
        elif behind == 4 and not other:
            ok = j > i + jnp.where(chip >= behind, 0, rows)
        elif behind == 4:
            ok = j < jnp.where((chip >= behind) & (core == 0), rows, 0)
        else:
            ok = j < jnp.where(chip >= behind, rows, 0)
        bias[:, n * rows : (n + 1) * rows] = jnp.where((theirs == mine) & ok, 0.0, FAR)
    v_all[:, HEAD:] = jnp.ones((count * rows, HEAD), BF16)
    group = q_ref.shape[2] // HEAD // KV_HEADS

    def one(head, _):
        here = lanes(head, HEAD)
        for n in range(count):
            k_all[n * rows : (n + 1) * rows, :] = pieces[n][0:rows, here]
            v_all[n * rows : (n + 1) * rows, 0:HEAD] = pieces[n][rows : 2 * rows, here]
        for layer in range(2):
            for r in range(group):
                cols = lanes(head * group + r, HEAD)
                scores = nt_dot(q_ref[layer, :, cols], k_all[...]) * SCALE + bias[...]
                peak = jnp.max(scores, axis=1, keepdims=True)
                if first:
                    probs = jnp.exp2(scores - peak)
                else:
                    old = peak_in[layer, :, cols]
                    peak = jnp.maximum(old, peak)
                    fade = jnp.exp2(old - peak)
                    probs = jnp.concatenate(
                        [
                            jnp.exp2(scores[:, n * rows : (n + 1) * rows] - peak)
                            for n in range(count)
                        ],
                        axis=1,
                    )
                both = jnp.dot(probs.astype(BF16), v_all[...], preferred_element_type=F32)
                acc = both[:, :HEAD]
                total = both[:, HEAD:]
                if not first:
                    acc = acc + fade * acc_in[layer, :, cols]
                    total = total + fade * sum_in[layer, :, cols]
                if last:
                    out_ref[layer, :, cols] = (acc / total).astype(BF16)
                else:
                    acc_out[layer, :, cols] = acc
                    sum_out[layer, :, cols] = total
                    peak_out[layer, :, cols] = jnp.broadcast_to(peak, (rows, HEAD))
        return _

    lax.fori_loop(0, KV_HEADS, one, 0)


def attend(place, queries, own, pieces, kinds, carry, last):
    layers, tokens, width = queries.shape
    count = len(kinds)
    partial = shaped(layers, tokens, width, dtype=F32)
    return call(
        functools.partial(attend_kernel, kinds, carry is None, last),
        "attend%d" % kinds[-1][0],
        0.5 + 1.05 * count,
        place,
        [queries, own] + list(pieces) + list(carry or ()),
        shaped(layers, tokens, width) if last else (partial,) * 3,
        [
            VMEM((count * tokens, HEAD), BF16),
            VMEM((count * tokens, 2 * HEAD), BF16),
            VMEM((tokens, count * tokens), F32),
        ],
    )


def spread(columns, pairs, width):
    low = lax.broadcasted_iota(jnp.int32, (1, 2 * width), 1) < width
    parts = [
        jnp.where(low, columns[:, 2 * k : 2 * k + 1], columns[:, 2 * k + 1 : 2 * k + 2])
        for k in range(pairs)
    ]
    return jnp.concatenate(parts, axis=1)


def put_logs(ref, state, logs):
    one = logs.astype(BF16)
    rest = logs - one.astype(F32)
    two = rest.astype(BF16)
    three = (rest - two.astype(F32)).astype(BF16)
    row = lax.broadcasted_iota(jnp.int32, (LOGS, logs.shape[1]), 0)
    ref[state:, :] = jnp.where(row == 0, one, jnp.where(row == 1, two, three))


def get_logs(ref, state):
    parts = ref[state:, :].astype(F32)
    return parts[0:1] + parts[1:2] + parts[2:3]


def local_kernel(
    heads, state, place, own_ref, c_ref, rate_ref, mixed_ref, mine_ref, give_ref, run_ref, read_ref,
    xs, tail
):
    tokens = own_ref.shape[0]
    cols = mixed_ref.shape[2]
    width = cols // heads
    core = place[0]
    xs[core] = own_ref[...]
    xs[1 - core] = c_ref[...]
    i = lax.broadcasted_iota(jnp.int32, (tokens, tokens), 0)
    j = lax.broadcasted_iota(jnp.int32, (tokens, tokens), 1)
    causal = j <= i
    lower_ones = causal.astype(F32)
    upper_ones = (i <= j).astype(F32)
    low = lax.broadcasted_iota(jnp.int32, (1, 2 * width), 1) < width
    rates = rate_ref[...]
    shift = lax.rem(128 - core * heads, 128)
    kept = None
    offset = None
    for b in range(2):
        write = xs[b, :, cols : cols + state]
        read = xs[b, :, cols + state : cols + 2 * state]
        read_ref[b] = read
        high = xs[b, :, cols + 2 * state :].astype(F32)
        little = pltpu.roll(high, 64, 1)
        level = jnp.floor(high * 0.0625)
        lower = high * 64.0 + little - 1024.0 * level
        step = -rates * (1.0 + lower * (1.0 / 128.0)) - 0.125 * level
        step = jnp.where(j < heads, pltpu.roll(step, shift, 1), 0.0)
        run = jnp.dot(
            lower_ones, step, preferred_element_type=F32, precision=lax.Precision.HIGHEST
        )
        run_t = tn_dot(step, upper_ones, lax.Precision.HIGHEST)
        end = run[tokens - 1 : tokens, :]
        run_ref[b] = run if b == 0 else run + offset
        offset = end if b == 0 else offset + end
        inner = jnp.where(causal, nt_dot(read, write), 0.0)
        to_end = jnp.exp(end - run)
        fade = jnp.exp(run)
        if b > 0:
            seen = jnp.dot(read, kept.astype(BF16), preferred_element_type=F32)
        scaled = []
        for pair in range(heads // 2):
            part = slice(pair * 2 * width, (pair + 1) * 2 * width)
            tile = xs[b, :, part]
            mixes = []
            for h in (2 * pair, 2 * pair + 1):
                gap = jnp.minimum(run[:, h : h + 1] - run_t[h : h + 1, :], 0.0)
                mixes.append((inner * jnp.exp(gap)).astype(BF16))
            zero = jnp.zeros_like(tile)
            stacked = jnp.concatenate(
                [jnp.where(low, tile, zero), jnp.where(low, zero, tile)], axis=0
            )
            mixed = jnp.dot(jnp.concatenate(mixes, axis=1), stacked, preferred_element_type=F32)
            if b > 0:
                mixed = mixed + seen[:, part] * jnp.where(
                    low, fade[:, 2 * pair : 2 * pair + 1], fade[:, 2 * pair + 1 : 2 * pair + 2]
                )
            mixed_ref[b, :, part] = mixed
            weight = jnp.where(
                low, to_end[:, 2 * pair : 2 * pair + 1], to_end[:, 2 * pair + 1 : 2 * pair + 2]
            )
            scaled.append((weight * tile.astype(F32)).astype(BF16))
        added = tn_dot(write, jnp.concatenate(scaled, axis=1))
        if b > 0:
            added = spread(jnp.exp(end), heads // 2, width) * kept + added
        kept = added
    tail[0:state, :] = kept.astype(BF16)
    put_logs(tail, state, spread(offset, heads // 2, width))
    y = place[1]
    mine_ref[...] = tail[:, lanes(y, cols // 2)]
    give_ref[...] = tail[:, lanes(1 - y, cols // 2)]


def row_kernel(state, place, tail_ref, y_ref, span_ref, first_ref):
    first = place[1] == 0
    mine = tail_ref[0:state, :].astype(F32)
    theirs = y_ref[0:state, :].astype(F32)
    my_log = get_logs(tail_ref, state)
    their_log = get_logs(y_ref, state)
    later = jnp.where(first, theirs, mine)
    earlier = jnp.where(first, mine, theirs)
    decay = jnp.exp(jnp.where(first, their_log, my_log))
    span_ref[0:state, :] = (later + decay * earlier).astype(BF16)
    put_logs(span_ref, state, my_log + their_log)
    first_ref[...] = jnp.where(first, tail_ref[...].astype(F32), y_ref[...].astype(F32)).astype(BF16)


def join(state, old_ref, new, new_logs):
    if old_ref is None:
        return new, new_logs
    logs = get_logs(old_ref, state)
    return old_ref[0:state, :].astype(F32) + jnp.exp(logs) * new, logs + new_logs


def hop_kernel(state, distance, last, place, *refs):
    refs = list(refs)
    span_ref = refs.pop(0)
    before_ref = refs.pop(0) if distance > 1 else None
    new_ref = refs.pop(0)
    ok = place[2] >= distance
    new = jnp.where(ok, new_ref[0:state, :].astype(F32), 0.0)
    new_logs = jnp.where(ok, get_logs(new_ref, state), 0.0)
    before, before_logs = join(state, before_ref, new, new_logs)
    if last:
        first_ref, keep_ref, give_ref = refs
        second, _ = join(state, first_ref, before, before_logs)
        y = place[1]
        keep_ref[...] = jnp.where(y == 0, before, second).astype(BF16)
        give_ref[...] = jnp.where(y == 0, second, before).astype(BF16)
    else:
        span_out, before_out = refs
        span, span_logs = join(state, span_ref, new, new_logs)
        span_out[0:state, :] = span.astype(BF16)
        put_logs(span_out, state, span_logs)
        before_out[0:state, :] = before.astype(BF16)
        put_logs(before_out, state, before_logs)


def finish_kernel(
    heads, state, place, mixed_ref, run_ref, read_ref, mine_ref, other_ref, self_ref, c_ref
):
    core = place[0]
    y = place[1]
    cols = mixed_ref.shape[2]
    width = cols // heads
    mine = mine_ref[...]
    other = other_ref[...]
    entering = jnp.concatenate(
        [jnp.where(y == 0, mine, other), jnp.where(y == 0, other, mine)], axis=1
    )
    a = lax.broadcasted_iota(jnp.int32, (4 * width, 2 * width), 0)
    b = lax.broadcasted_iota(jnp.int32, (4 * width, 2 * width), 1)
    same = (lax.rem(a, 2 * width) < width) == (b < width)
    average = jnp.where(same, 1.0 / width, 0.0).astype(BF16)
    low = lax.broadcasted_iota(jnp.int32, (1, 2 * width), 1) < width
    for out_ref, at in ((c_ref, 1 - core), (self_ref, core)):
        seen = jnp.dot(read_ref[at], entering, preferred_element_type=F32)
        fade = jnp.exp(run_ref[at])
        for pair in range(heads // 2):
            part = slice(pair * 2 * width, (pair + 1) * 2 * width)
            tile = mixed_ref[at, :, part] + seen[:, part] * jnp.where(
                low, fade[:, 2 * pair : 2 * pair + 1], fade[:, 2 * pair + 1 : 2 * pair + 2]
            )
            square = tile * tile
            big = square.astype(BF16)
            small = (square - big.astype(F32)).astype(BF16)
            mean = jnp.dot(
                jnp.concatenate([big, small], axis=1), average, preferred_element_type=F32
            )
            out_ref[:, part] = (tile * lax.rsqrt(mean + 1e-05)).astype(BF16)


def collect_kernel(place, self_ref, c_ref, out_ref):
    core = place[0]
    cols = self_ref.shape[1]
    out_ref[:, lanes(core, cols)] = self_ref[...]
    out_ref[:, lanes(1 - core, cols)] = c_ref[...]


def after(value, *others):
    return lax.optimization_barrier((value, *others))[0]


def shards(
    ssm_inputs, state_write, state_read, decay_codes, decay_rate, queries, keys_values, segment_ids
):
    tokens, channels = ssm_inputs.shape
    heads = decay_rate.shape[0]
    state = state_write.shape[1]
    cols = channels // 2
    devices = lax.axis_size("seq")
    rows = devices // ROW
    rank = lax.axis_index("seq")
    core, y = rank % 2, (rank // 2) % 2
    place = jnp.stack([core, y, rank // ROW, rank // 2]).astype(jnp.int32)
    send = lambda x, route: lax.ppermute(x, "seq", [(i, route(i)) for i in range(devices)])
    swap_c = lambda i: i ^ 1
    swap_y = lambda i: i ^ 2
    up = lambda n: lambda i: (i + n * ROW) % devices
    kv_width = keys_values.shape[2]
    half = cols // 2

    own, mine, to_c, rates = call(
        pack_kernel,
        "pack",
        1.5,
        place,
        [
            ssm_inputs,
            state_write,
            state_read,
            decay_codes.T,
            keys_values,
            segment_ids[None, :],
            decay_rate[None, :],
        ],
        (
            shaped(2 * tokens + 16, kv_width),
            shaped(tokens, cols + 2 * state + 128),
            shaped(tokens, cols + 2 * state + 128),
            shaped(1, 128, dtype=F32),
        ),
        [
            VMEM((heads, tokens), jnp.int32),
            VMEM((1, tokens), jnp.int32),
            VMEM((1, heads), F32),
            pltpu.SemaphoreType.DMA((11,)),
        ],
        True,
    )
    from_c = send(to_c, swap_c)
    behind2 = send(own, up(1))
    partner = send(own, swap_c)

    mixed, tail, tail_out, run, reads = call(
        functools.partial(local_kernel, heads // 2, state),
        "local",
        4.3,
        place,
        [mine, from_c, rates],
        (
            shaped(2, tokens, cols, dtype=F32),
            shaped(state + LOGS, half),
            shaped(state + LOGS, half),
            shaped(2, tokens, 128, dtype=F32),
            shaped(2, tokens, state),
        ),
        [
            VMEM((2, tokens, cols + 2 * state + 128), BF16),
            VMEM((state + LOGS, cols), BF16),
        ],
    )
    tail_y = send(tail_out, swap_y)
    carry = attend(
        place, after(queries, tail), own, [own, partner], ((0, False), (0, True)), None, False
    )
    tail_y = after(tail_y, carry[0])
    span, first = call(
        functools.partial(row_kernel, state),
        "row",
        0.6,
        place,
        [tail, tail_y],
        (shaped(state + LOGS, half),) * 2,
    )
    new = send(span, up(1))
    behind2 = after(behind2, span)
    behind4 = send(behind2, up(1))
    to_y = jnp.where(y == 0, own, behind2)
    behind1 = send(to_y, swap_y)
    behind2c = send(behind2, swap_c)
    carry = attend(
        place,
        lax.optimization_barrier((queries, span, to_y))[0],
        own,
        [behind2, behind2c],
        ((2, False), (2, True)),
        carry,
        False,
    )
    new = after(new, carry[0])
    behind4, behind1 = after(behind4, carry[0]), after(behind1, carry[0])

    to_y = jnp.where(y == 0, behind2, behind4)
    behind3 = send(to_y, swap_y)
    behind1c = send(behind1, swap_c)
    behind4c = send(behind4, swap_c)
    before = None
    distance = 1
    while distance < rows:
        last = 2 * distance >= rows
        out = call(
            functools.partial(hop_kernel, state, distance, last),
            "hop%d" % distance,
            0.6,
            place,
            [span] + [before] * (distance > 1) + [new] + [first] * last,
            (shaped(state, half) if last else shaped(state + LOGS, half),) * 2,
        )
        if last:
            keep, give = out
        else:
            span, before = out
            new = send(span, up(2 * distance))
        if distance == 1:
            carry = attend(
                place,
                lax.optimization_barrier((queries, span, to_y))[0],
                own,
                [behind1, behind1c, behind4, behind4c],
                ((1, False), (1, True), (4, False), (4, True)),
                carry,
                False,
            )
            new, behind3 = after(new, carry[0]), after(behind3, carry[0])
            behind3c = send(behind3, swap_c)
        distance *= 2
    other_half = send(give, swap_y)
    done, for_c = call(
        functools.partial(finish_kernel, heads // 2, state),
        "finish",
        1.7,
        place,
        [mixed, run, reads, keep, other_half],
        (shaped(tokens, cols),) * 2,
    )
    back_c = send(for_c, swap_c)
    attn_output = attend(
        place,
        after(queries, for_c),
        own,
        [behind3, behind3c],
        ((3, False), (3, True)),
        carry,
        True,
    )
    ssm_output = call(
        collect_kernel,
        "collect",
        0.8,
        place,
        [done, after(back_c, attn_output)],
        shaped(tokens, channels),
    )
    return (ssm_output, attn_output)


def solution(mesh):
    return jax.shard_map(
        shards,
        mesh=mesh,
        in_specs=(
            P(("groups", "seq"), None),
            P(("groups", "seq"), None),
            P(("groups", "seq"), None),
            P(("groups", "seq"), None),
            P(),
            P(None, ("groups", "seq"), None),
            P(None, ("groups", "seq"), None),
            P(("groups", "seq")),
        ),
        out_specs=(P(("groups", "seq"), None), P(None, ("groups", "seq"), None)),
        check_vma=False,
    )
```

```python
import functools
import math

import jax
import jax.numpy as jnp
from jax import lax
from jax.experimental import pallas as pl
from jax.experimental.pallas import tpu as pltpu
from jax.sharding import PartitionSpec as P

KV_HEADS = 4
HEAD = 128
ROW = 4
FAR = -1e30
SCALE = HEAD ** (-0.5) * math.log2(math.e)
F32 = jnp.float32
BF16 = jnp.bfloat16
VMEM = pltpu.VMEM
IN_SMEM = pl.BlockSpec(memory_space=pltpu.SMEM)
IN_VMEM = pl.BlockSpec(memory_space=pltpu.VMEM)
LOGS = 16


def nt_dot(a, b):
    return lax.dot_general(a, b, (((1,), (1,)), ((), ())), preferred_element_type=F32)


def tn_dot(a, b, precision=None):
    return lax.dot_general(
        a, b, (((0,), (0,)), ((), ())), preferred_element_type=F32, precision=precision
    )


def lanes(number, width):
    return pl.ds(pl.multiple_of(number * width, width), width)


def call(kernel, name, micros, place, args, outs, scratch=(), stay=False, mib=8):
    spec = pl.BlockSpec(memory_space=pltpu.HBM) if stay else IN_VMEM
    return pl.pallas_call(
        kernel,
        name=name,
        out_shape=outs,
        in_specs=[IN_SMEM] + [spec] * len(args),
        out_specs=jax.tree.map(lambda _: IN_VMEM, outs),
        scratch_shapes=list(scratch),
        cost_estimate=pl.CostEstimate(
            flops=int(micros * 1.15e9), bytes_accessed=0, transcendentals=0
        ),
        compiler_params=pltpu.CompilerParams(vmem_limit_bytes=mib * 1024 * 1024),
    )(place, *[pltpu.with_memory_space_constraint(a, pltpu.HBM) if stay else a for a in args])


def shaped(*shape, dtype=BF16):
    return jax.ShapeDtypeStruct(shape, dtype)


def pack_kernel(
    place, x, write, read, codes, kv, seg, rate, own, mine, to_c, rates, code_buf, seg_buf, rate_buf,
    sems
):
    core = place[0]
    tokens, state = write.shape
    heads = codes.shape[0]
    half = x.shape[1] // 2
    copies = [
        (kv.at[0], own.at[0:tokens]),
        (kv.at[1], own.at[tokens : 2 * tokens]),
        (x.at[:, lanes(1 - core, half)], to_c.at[:, 0:half]),
        (write, to_c.at[:, half : half + state]),
        (read, to_c.at[:, half + state : half + 2 * state]),
        (codes, code_buf),
        (seg, seg_buf),
        (rate, rate_buf),
        (x.at[:, lanes(core, half)], mine.at[:, 0:half]),
        (write, mine.at[:, half : half + state]),
        (read, mine.at[:, half + state : half + 2 * state]),
    ]
    copies = [
        pltpu.make_async_copy(source, target, sems.at[n])
        for n, (source, target) in enumerate(copies)
    ]
    for copy in copies:
        copy.start()
    own[2 * tokens :, tokens:] = jnp.zeros((16, own.shape[1] - tokens), BF16)
    for copy in copies:
        copy.wait()
    codes_of = (seg_buf[...] + 1).astype(F32).astype(BF16)
    own[2 * tokens :, 0:tokens] = jnp.broadcast_to(codes_of, (16, tokens))
    code = code_buf[...]
    high = (code >> 6).astype(F32)
    low = (code & 63).astype(F32)
    gap = jnp.zeros((64 - heads, tokens), F32)
    both = jnp.transpose(jnp.concatenate([high, gap, low, gap], axis=0)).astype(BF16)
    mine[:, half + 2 * state :] = both
    to_c[:, half + 2 * state :] = both
    rates[...] = jnp.concatenate([rate_buf[...], jnp.zeros((1, 128 - heads), F32)], axis=1)


def attend_kernel(kinds, first, last, place, q_ref, own_ref, *refs):
    count = len(kinds)
    rows = q_ref.shape[1]
    pieces = refs[:count]
    at = count
    if not first:
        acc_in, peak_in, sum_in = refs[at : at + 3]
        at += 3
    if last:
        out_ref = refs[at]
        at += 1
    else:
        acc_out, peak_out, sum_out = refs[at : at + 3]
        at += 3
    k_all, v_all, bias = refs[at : at + 3]
    core = place[0]
    chip = place[3]
    codes = own_ref[2 * rows : 2 * rows + 16, 0:rows].astype(F32)
    mine = jnp.transpose(jnp.broadcast_to(codes[0:1], (rows, rows)))
    i = lax.broadcasted_iota(jnp.int32, (rows, rows), 0)
    j = lax.broadcasted_iota(jnp.int32, (rows, rows), 1)
    for n, (behind, other) in enumerate(kinds):
        theirs = pieces[n][2 * rows : 2 * rows + 16, 0:rows].astype(F32)[0:1]
        if behind == 0 and not other:
            ok = j <= i
        elif behind == 0:
            ok = j < rows * core
        elif behind == 4 and not other:
            ok = j > i + jnp.where(chip >= behind, 0, rows)
        elif behind == 4:
            ok = j < jnp.where((chip >= behind) & (core == 0), rows, 0)
        else:
            ok = j < jnp.where(chip >= behind, rows, 0)
        bias[:, n * rows : (n + 1) * rows] = jnp.where((theirs == mine) & ok, 0.0, FAR)
    v_all[:, HEAD:] = jnp.ones((count * rows, HEAD), BF16)
    group = q_ref.shape[2] // HEAD // KV_HEADS

    def one(head, _):
        here = lanes(head, HEAD)
        for n in range(count):
            k_all[n * rows : (n + 1) * rows, :] = pieces[n][0:rows, here]
            v_all[n * rows : (n + 1) * rows, 0:HEAD] = pieces[n][rows : 2 * rows, here]
        for layer in range(2):
            for r in range(group):
                cols = lanes(head * group + r, HEAD)
                scores = nt_dot(q_ref[layer, :, cols], k_all[...]) * SCALE + bias[...]
                peak = jnp.max(scores, axis=1, keepdims=True)
                if first:
                    probs = jnp.exp2(scores - peak)
                else:
                    old = peak_in[layer, :, cols]
                    peak = jnp.maximum(old, peak)
                    fade = jnp.exp2(old - peak)
                    probs = jnp.concatenate(
                        [
                            jnp.exp2(scores[:, n * rows : (n + 1) * rows] - peak)
                            for n in range(count)
                        ],
                        axis=1,
                    )
                both = jnp.dot(probs.astype(BF16), v_all[...], preferred_element_type=F32)
                acc = both[:, :HEAD]
                total = both[:, HEAD:]
                if not first:
                    acc = acc + fade * acc_in[layer, :, cols]
                    total = total + fade * sum_in[layer, :, cols]
                if last:
                    out_ref[layer, :, cols] = (acc / total).astype(BF16)
                else:
                    acc_out[layer, :, cols] = acc
                    sum_out[layer, :, cols] = total
                    peak_out[layer, :, cols] = jnp.broadcast_to(peak, (rows, HEAD))
        return _

    lax.fori_loop(0, KV_HEADS, one, 0)


def attend(place, queries, own, pieces, kinds, carry, last):
    layers, tokens, width = queries.shape
    count = len(kinds)
    partial = shaped(layers, tokens, width, dtype=F32)
    return call(
        functools.partial(attend_kernel, kinds, carry is None, last),
        "attend%d" % kinds[-1][0],
        0.5 + 1.05 * count,
        place,
        [queries, own]
        + list(pieces)
        + [pltpu.with_memory_space_constraint(part, pltpu.VMEM) for part in carry or ()],
        shaped(layers, tokens, width) if last else (partial,) * 3,
        [
            VMEM((count * tokens, HEAD), BF16),
            VMEM((count * tokens, 2 * HEAD), BF16),
            VMEM((tokens, count * tokens), F32),
        ],
        mib=20,
    )


def spread(columns, pairs, width):
    low = lax.broadcasted_iota(jnp.int32, (1, 2 * width), 1) < width
    parts = [
        jnp.where(low, columns[:, 2 * k : 2 * k + 1], columns[:, 2 * k + 1 : 2 * k + 2])
        for k in range(pairs)
    ]
    return jnp.concatenate(parts, axis=1)


def put_logs(ref, state, logs):
    one = logs.astype(BF16)
    rest = logs - one.astype(F32)
    two = rest.astype(BF16)
    three = (rest - two.astype(F32)).astype(BF16)
    row = lax.broadcasted_iota(jnp.int32, (LOGS, logs.shape[1]), 0)
    ref[state:, :] = jnp.where(row == 0, one, jnp.where(row == 1, two, three))


def get_logs(ref, state):
    parts = ref[state:, :].astype(F32)
    return parts[0:1] + parts[1:2] + parts[2:3]


def local_kernel(
    heads, state, place, own_ref, c_ref, rate_ref, mixed_ref, mine_ref, give_ref, run_ref, read_ref,
    xs, tail
):
    tokens = own_ref.shape[0]
    cols = mixed_ref.shape[2]
    width = cols // heads
    core = place[0]
    xs[core] = own_ref[...]
    xs[1 - core] = c_ref[...]
    i = lax.broadcasted_iota(jnp.int32, (tokens, tokens), 0)
    j = lax.broadcasted_iota(jnp.int32, (tokens, tokens), 1)
    causal = j <= i
    lower_ones = causal.astype(F32)
    upper_ones = (i <= j).astype(F32)
    low = lax.broadcasted_iota(jnp.int32, (1, 2 * width), 1) < width
    rates = rate_ref[...]
    shift = lax.rem(128 - core * heads, 128)
    kept = None
    offset = None
    for b in range(2):
        write = xs[b, :, cols : cols + state]
        read = xs[b, :, cols + state : cols + 2 * state]
        read_ref[b] = read
        high = xs[b, :, cols + 2 * state :].astype(F32)
        little = pltpu.roll(high, 64, 1)
        level = jnp.floor(high * 0.0625)
        lower = high * 64.0 + little - 1024.0 * level
        step = -rates * (1.0 + lower * (1.0 / 128.0)) - 0.125 * level
        step = jnp.where(j < heads, pltpu.roll(step, shift, 1), 0.0)
        run = jnp.dot(
            lower_ones, step, preferred_element_type=F32, precision=lax.Precision.HIGHEST
        )
        run_t = tn_dot(step, upper_ones, lax.Precision.HIGHEST)
        end = run[tokens - 1 : tokens, :]
        run_ref[b] = run if b == 0 else run + offset
        offset = end if b == 0 else offset + end
        inner = jnp.where(causal, nt_dot(read, write), 0.0)
        to_end = jnp.exp(end - run)
        fade = jnp.exp(run)
        if b > 0:
            seen = jnp.dot(read, kept.astype(BF16), preferred_element_type=F32)
        scaled = []
        for pair in range(heads // 2):
            part = slice(pair * 2 * width, (pair + 1) * 2 * width)
            tile = xs[b, :, part]
            mixes = []
            for h in (2 * pair, 2 * pair + 1):
                gap = jnp.minimum(run[:, h : h + 1] - run_t[h : h + 1, :], 0.0)
                mixes.append((inner * jnp.exp(gap)).astype(BF16))
            zero = jnp.zeros_like(tile)
            stacked = jnp.concatenate(
                [jnp.where(low, tile, zero), jnp.where(low, zero, tile)], axis=0
            )
            mixed = jnp.dot(jnp.concatenate(mixes, axis=1), stacked, preferred_element_type=F32)
            if b > 0:
                mixed = mixed + seen[:, part] * jnp.where(
                    low, fade[:, 2 * pair : 2 * pair + 1], fade[:, 2 * pair + 1 : 2 * pair + 2]
                )
            mixed_ref[b, :, part] = mixed
            weight = jnp.where(
                low, to_end[:, 2 * pair : 2 * pair + 1], to_end[:, 2 * pair + 1 : 2 * pair + 2]
            )
            scaled.append((weight * tile.astype(F32)).astype(BF16))
        added = tn_dot(write, jnp.concatenate(scaled, axis=1))
        if b > 0:
            added = spread(jnp.exp(end), heads // 2, width) * kept + added
        kept = added
    tail[0:state, :] = kept.astype(BF16)
    put_logs(tail, state, spread(offset, heads // 2, width))
    y = place[1]
    mine_ref[...] = tail[:, lanes(y, cols // 2)]
    give_ref[...] = tail[:, lanes(1 - y, cols // 2)]


def pick(place, low_ref, high_ref, out_ref):
    @pl.when(place[1] == 0)
    def _():
        out_ref[...] = low_ref[...]

    @pl.when(place[1] != 0)
    def _():
        out_ref[...] = high_ref[...]


def row_kernel(state, place, tail_ref, y_ref, low_ref, high_ref, span_ref, first_ref, to_y):
    pick(place, low_ref, high_ref, to_y)
    first = place[1] == 0
    mine = tail_ref[0:state, :].astype(F32)
    theirs = y_ref[0:state, :].astype(F32)
    my_log = get_logs(tail_ref, state)
    their_log = get_logs(y_ref, state)
    later = jnp.where(first, theirs, mine)
    earlier = jnp.where(first, mine, theirs)
    decay = jnp.exp(jnp.where(first, their_log, my_log))
    span_ref[0:state, :] = (later + decay * earlier).astype(BF16)
    put_logs(span_ref, state, my_log + their_log)
    first_ref[...] = jnp.where(first, tail_ref[...].astype(F32), y_ref[...].astype(F32)).astype(BF16)


def join(state, old_ref, new, new_logs):
    if old_ref is None:
        return new, new_logs
    logs = get_logs(old_ref, state)
    return old_ref[0:state, :].astype(F32) + jnp.exp(logs) * new, logs + new_logs


def hop_kernel(state, distance, last, place, *refs):
    refs = list(refs)
    span_ref = refs.pop(0)
    before_ref = refs.pop(0) if distance > 1 else None
    new_ref = refs.pop(0)
    ok = place[2] >= distance
    new = jnp.where(ok, new_ref[0:state, :].astype(F32), 0.0)
    new_logs = jnp.where(ok, get_logs(new_ref, state), 0.0)
    before, before_logs = join(state, before_ref, new, new_logs)
    if last:
        first_ref, keep_ref, give_ref = refs
        second, _ = join(state, first_ref, before, before_logs)
        y = place[1]
        keep_ref[...] = jnp.where(y == 0, before, second).astype(BF16)
        give_ref[...] = jnp.where(y == 0, second, before).astype(BF16)
    else:
        span_out, before_out = refs
        span, span_logs = join(state, span_ref, new, new_logs)
        span_out[0:state, :] = span.astype(BF16)
        put_logs(span_out, state, span_logs)
        before_out[0:state, :] = before.astype(BF16)
        put_logs(before_out, state, before_logs)


def finish_kernel(
    heads, state, place, mixed_ref, run_ref, read_ref, mine_ref, other_ref, self_ref, c_ref
):
    core = place[0]
    y = place[1]
    cols = mixed_ref.shape[2]
    width = cols // heads
    mine = mine_ref[...]
    other = other_ref[...]
    entering = jnp.concatenate(
        [jnp.where(y == 0, mine, other), jnp.where(y == 0, other, mine)], axis=1
    )
    a = lax.broadcasted_iota(jnp.int32, (4 * width, 2 * width), 0)
    b = lax.broadcasted_iota(jnp.int32, (4 * width, 2 * width), 1)
    same = (lax.rem(a, 2 * width) < width) == (b < width)
    average = jnp.where(same, 1.0 / width, 0.0).astype(BF16)
    low = lax.broadcasted_iota(jnp.int32, (1, 2 * width), 1) < width
    for out_ref, at in ((c_ref, 1 - core), (self_ref, core)):
        seen = jnp.dot(read_ref[at], entering, preferred_element_type=F32)
        fade = jnp.exp(run_ref[at])
        for pair in range(heads // 2):
            part = slice(pair * 2 * width, (pair + 1) * 2 * width)
            tile = mixed_ref[at, :, part] + seen[:, part] * jnp.where(
                low, fade[:, 2 * pair : 2 * pair + 1], fade[:, 2 * pair + 1 : 2 * pair + 2]
            )
            square = tile * tile
            big = square.astype(BF16)
            small = (square - big.astype(F32)).astype(BF16)
            mean = jnp.dot(
                jnp.concatenate([big, small], axis=1), average, preferred_element_type=F32
            )
            out_ref[:, part] = (tile * lax.rsqrt(mean + 1e-05)).astype(BF16)


def collect_kernel(place, self_ref, c_ref, out_ref):
    core = place[0]
    cols = self_ref.shape[1]
    out_ref[:, lanes(core, cols)] = self_ref[...]
    out_ref[:, lanes(1 - core, cols)] = c_ref[...]


def after(value, *others):
    return lax.optimization_barrier((value, *others))[0]


def shards(
    ssm_inputs, state_write, state_read, decay_codes, decay_rate, queries, keys_values, segment_ids
):
    tokens, channels = ssm_inputs.shape
    heads = decay_rate.shape[0]
    state = state_write.shape[1]
    cols = channels // 2
    devices = lax.axis_size("seq")
    rows = devices // ROW
    rank = lax.axis_index("seq")
    core, y = rank % 2, (rank // 2) % 2
    place = jnp.stack([core, y, rank // ROW, rank // 2]).astype(jnp.int32)
    send = lambda x, route: lax.ppermute(x, "seq", [(i, route(i)) for i in range(devices)])
    swap_c = lambda i: i ^ 1
    swap_y = lambda i: i ^ 2
    up = lambda n: lambda i: (i + n * ROW) % devices
    kv_width = keys_values.shape[2]
    half = cols // 2

    own, mine, to_c, rates = call(
        pack_kernel,
        "pack",
        1.5,
        place,
        [
            ssm_inputs,
            state_write,
            state_read,
            decay_codes.T,
            keys_values,
            segment_ids[None, :],
            decay_rate[None, :],
        ],
        (
            shaped(2 * tokens + 16, kv_width),
            shaped(tokens, cols + 2 * state + 128),
            shaped(tokens, cols + 2 * state + 128),
            shaped(1, 128, dtype=F32),
        ),
        [
            VMEM((heads, tokens), jnp.int32),
            VMEM((1, tokens), jnp.int32),
            VMEM((1, heads), F32),
            pltpu.SemaphoreType.DMA((11,)),
        ],
        True,
    )
    from_c = send(to_c, swap_c)
    behind2 = send(own, up(1))
    partner = send(own, swap_c)

    mixed, tail, tail_out, run, reads = call(
        functools.partial(local_kernel, heads // 2, state),
        "local",
        4.3,
        place,
        [mine, from_c, rates],
        (
            shaped(2, tokens, cols, dtype=F32),
            shaped(state + LOGS, half),
            shaped(state + LOGS, half),
            shaped(2, tokens, 128, dtype=F32),
            shaped(2, tokens, state),
        ),
        [
            VMEM((2, tokens, cols + 2 * state + 128), BF16),
            VMEM((state + LOGS, cols), BF16),
        ],
    )
    tail_y = send(tail_out, swap_y)
    carry = attend(
        place, after(queries, tail), own, [own, partner], ((0, False), (0, True)), None, False
    )
    tail_y = after(tail_y, carry[0])
    span, first, to_y = call(
        functools.partial(row_kernel, state),
        "row",
        20.0,
        place,
        [tail, tail_y, own, behind2],
        (shaped(state + LOGS, half),) * 2 + (shaped(2 * tokens + 16, kv_width),),
    )
    new = send(span, up(1))
    behind2 = after(behind2, span)
    behind4 = send(behind2, up(1))
    behind1 = send(to_y, swap_y)
    behind2c = send(behind2, swap_c)
    before = None
    distance = 1
    while distance < rows:
        last = 2 * distance >= rows
        out = call(
            functools.partial(hop_kernel, state, distance, last),
            "hop%d" % distance,
            20.0,
            place,
            [span] + [before] * (distance > 1) + [new] + [first] * last,
            (shaped(state, half) if last else shaped(state + LOGS, half),) * 2,
        )
        if last:
            keep, give = out
        else:
            span, before = out
            new = send(span, up(2 * distance))
        if distance == 1:
            carry = attend(
                place,
                after(queries, before),
                own,
                [behind2, behind2c],
                ((2, False), (2, True)),
                carry,
                False,
            )
            behind4, behind1 = after(behind4, carry[0]), after(behind1, carry[0])
            behind1c = send(behind1, swap_c)
            behind4c = send(behind4, swap_c)
            to_y = call(
                pick,
                "pick",
                20.0,
                place,
                [behind2, behind4],
                shaped(2 * tokens + 16, kv_width),
            )
            behind3 = send(to_y, swap_y)
            new = after(new, to_y)
        distance *= 2
    carry = attend(
        place,
        after(queries, give),
        own,
        [behind1, behind1c, behind4, behind4c],
        ((1, False), (1, True), (4, False), (4, True)),
        carry,
        False,
    )
    behind3 = after(behind3, carry[0])
    behind3c = send(behind3, swap_c)
    other_half = after(send(give, swap_y), carry[0])
    done, for_c = call(
        functools.partial(finish_kernel, heads // 2, state),
        "finish",
        1.7,
        place,
        [mixed, run, reads, keep, other_half],
        (shaped(tokens, cols),) * 2,
    )
    back_c = send(for_c, swap_c)
    attn_output = attend(
        place,
        after(queries, for_c),
        own,
        [behind3, behind3c],
        ((3, False), (3, True)),
        carry,
        True,
    )
    ssm_output = call(
        collect_kernel,
        "collect",
        0.8,
        place,
        [done, after(back_c, attn_output)],
        shaped(tokens, channels),
    )
    return (ssm_output, attn_output)


def solution(mesh):
    return jax.shard_map(
        shards,
        mesh=mesh,
        in_specs=(
            P(("groups", "seq"), None),
            P(("groups", "seq"), None),
            P(("groups", "seq"), None),
            P(("groups", "seq"), None),
            P(),
            P(None, ("groups", "seq"), None),
            P(None, ("groups", "seq"), None),
            P(("groups", "seq")),
        ),
        out_specs=(P(("groups", "seq"), None), P(None, ("groups", "seq"), None)),
        check_vma=False,
    )
```

```python
import functools
import math

import jax
import jax.numpy as jnp
from jax import lax
from jax.experimental import pallas as pl
from jax.experimental.pallas import tpu as pltpu
from jax.sharding import PartitionSpec as P

KV_HEADS = 4
HEAD = 128
ROW = 4
FAR = -1e30
SCALE = HEAD ** (-0.5) * math.log2(math.e)
F32 = jnp.float32
BF16 = jnp.bfloat16
VMEM = pltpu.VMEM
IN_VMEM = pl.BlockSpec(memory_space=pltpu.VMEM)
LOGS = 16


def nt_dot(a, b):
    return lax.dot_general(a, b, (((1,), (1,)), ((), ())), preferred_element_type=F32)


def tn_dot(a, b, precision=None):
    return lax.dot_general(
        a, b, (((0,), (0,)), ((), ())), preferred_element_type=F32, precision=precision
    )


def lanes(number, width):
    return pl.ds(pl.multiple_of(number * width, width), width)


def call(kernel, name, micros, args, outs, scratch=(), stay=False, mib=8):
    spec = pl.BlockSpec(memory_space=pltpu.HBM) if stay else IN_VMEM

    def placed(*refs):
        rank = lax.axis_index("seq")
        kernel((rank & 1, (rank >> 1) & 1, rank >> 2, rank >> 1), *refs)

    return pl.pallas_call(
        placed,
        name=name,
        out_shape=outs,
        in_specs=[spec] * len(args),
        out_specs=jax.tree.map(lambda _: IN_VMEM, outs),
        scratch_shapes=list(scratch),
        cost_estimate=pl.CostEstimate(
            flops=int(micros * 1.15e9), bytes_accessed=0, transcendentals=0
        ),
        compiler_params=pltpu.CompilerParams(vmem_limit_bytes=mib * 1024 * 1024),
    )(*[pltpu.with_memory_space_constraint(a, pltpu.HBM) if stay else a for a in args])


def shaped(*shape, dtype=BF16):
    return jax.ShapeDtypeStruct(shape, dtype)


def pack_kernel(
    place, x, write, read, codes, kv, seg, rate, own, docs, mine, to_c, rates, code_buf, seg_buf, rate_buf,
    sems
):
    core = place[0]
    tokens, state = write.shape
    heads = codes.shape[0]
    half = x.shape[1] // 2
    copies = [
        (kv.at[0], own.at[0:tokens]),
        (kv.at[1], own.at[tokens : 2 * tokens]),
        (x.at[:, lanes(1 - core, half)], to_c.at[:, 0:half]),
        (write, to_c.at[:, half : half + state]),
        (read, to_c.at[:, half + state : half + 2 * state]),
        (codes, code_buf),
        (seg, seg_buf),
        (rate, rate_buf),
        (x.at[:, lanes(core, half)], mine.at[:, 0:half]),
        (write, mine.at[:, half : half + state]),
        (read, mine.at[:, half + state : half + 2 * state]),
    ]
    copies = [
        pltpu.make_async_copy(source, target, sems.at[n])
        for n, (source, target) in enumerate(copies)
    ]
    for copy in copies:
        copy.start()
    own[2 * tokens :, tokens:] = jnp.zeros((16, own.shape[1] - tokens), BF16)
    for copy in copies:
        copy.wait()
    codes_of = (seg_buf[...] + 1).astype(F32).astype(BF16)
    own[2 * tokens :, 0:tokens] = jnp.broadcast_to(codes_of, (16, tokens))
    docs[...] = jnp.transpose(jnp.broadcast_to(codes_of.astype(F32), (tokens, tokens)))
    code = code_buf[...]
    high = (code >> 6).astype(F32)
    low = (code & 63).astype(F32)
    gap = jnp.zeros((64 - heads, tokens), F32)
    both = jnp.transpose(jnp.concatenate([high, gap, low, gap], axis=0)).astype(BF16)
    mine[:, half + 2 * state :] = both
    to_c[:, half + 2 * state :] = both
    rates[...] = jnp.concatenate([rate_buf[...], jnp.zeros((1, 128 - heads), F32)], axis=1)


def attend_kernel(kinds, first, last, place, q_ref, doc_ref, *refs):
    count = len(kinds)
    rows = q_ref.shape[1]
    pieces = refs[:count]
    at = count
    if not first:
        acc_in, peak_in, sum_in = refs[at : at + 3]
        at += 3
    if last:
        out_ref = refs[at]
        at += 1
    else:
        acc_out, peak_out, sum_out = refs[at : at + 3]
        at += 3
    k_all, v_all, bias = refs[at : at + 3]
    core = place[0]
    chip = place[3]
    mine = doc_ref[...]
    i = lax.broadcasted_iota(jnp.int32, (rows, rows), 0)
    j = lax.broadcasted_iota(jnp.int32, (rows, rows), 1)
    for n, (behind, other) in enumerate(kinds):
        theirs = pieces[n][2 * rows : 2 * rows + 16, 0:rows].astype(F32)[0:1]
        if behind == 0 and not other:
            ok = j <= i
        elif behind == 0:
            ok = j < rows * core
        elif behind == 4 and not other:
            ok = j > i + jnp.where(chip >= behind, 0, rows)
        elif behind == 4:
            ok = j < jnp.where((chip >= behind) & (core == 0), rows, 0)
        else:
            ok = j < jnp.where(chip >= behind, rows, 0)
        bias[:, n * rows : (n + 1) * rows] = jnp.where((theirs == mine) & ok, 0.0, FAR)
    v_all[:, HEAD:] = jnp.ones((count * rows, HEAD), BF16)
    group = q_ref.shape[2] // HEAD // KV_HEADS

    def one(head, _):
        here = lanes(head, HEAD)
        for n in range(count):
            k_all[n * rows : (n + 1) * rows, :] = pieces[n][0:rows, here]
            v_all[n * rows : (n + 1) * rows, 0:HEAD] = pieces[n][rows : 2 * rows, here]
        for layer in range(2):
            for r in range(group):
                cols = lanes(head * group + r, HEAD)
                scores = nt_dot(q_ref[layer, :, cols], k_all[...]) * SCALE + bias[...]
                peak = jnp.max(scores, axis=1, keepdims=True)
                if first:
                    probs = jnp.exp2(scores - peak)
                else:
                    old = peak_in[layer, :, cols]
                    peak = jnp.maximum(old, peak)
                    fade = jnp.exp2(old - peak)
                    probs = jnp.concatenate(
                        [
                            jnp.exp2(scores[:, n * rows : (n + 1) * rows] - peak)
                            for n in range(count)
                        ],
                        axis=1,
                    )
                both = jnp.dot(probs.astype(BF16), v_all[...], preferred_element_type=F32)
                acc = both[:, :HEAD]
                total = both[:, HEAD:]
                if not first:
                    acc = acc + fade * acc_in[layer, :, cols]
                    total = total + fade * sum_in[layer, :, cols]
                if last:
                    out_ref[layer, :, cols] = (acc / total).astype(BF16)
                else:
                    acc_out[layer, :, cols] = acc
                    sum_out[layer, :, cols] = total
                    peak_out[layer, :, cols] = jnp.broadcast_to(peak, (rows, HEAD))
        return _

    lax.fori_loop(0, KV_HEADS, one, 0)


def attend(queries, docs, pieces, kinds, carry, last):
    layers, tokens, width = queries.shape
    count = len(kinds)
    partial = shaped(layers, tokens, width, dtype=F32)
    return call(
        functools.partial(attend_kernel, kinds, carry is None, last),
        "attend%d" % kinds[-1][0],
        0.5 + 1.05 * count,
        [queries, docs]
        + list(pieces)
        + [pltpu.with_memory_space_constraint(part, pltpu.VMEM) for part in carry or ()],
        shaped(layers, tokens, width) if last else (partial,) * 3,
        [
            VMEM((count * tokens, HEAD), BF16),
            VMEM((count * tokens, 2 * HEAD), BF16),
            VMEM((tokens, count * tokens), F32),
        ],
        mib=20,
    )


def spread(columns, pairs, width):
    low = lax.broadcasted_iota(jnp.int32, (1, 2 * width), 1) < width
    parts = [
        jnp.where(low, columns[:, 2 * k : 2 * k + 1], columns[:, 2 * k + 1 : 2 * k + 2])
        for k in range(pairs)
    ]
    return jnp.concatenate(parts, axis=1)


def put_logs(ref, state, logs):
    one = logs.astype(BF16)
    rest = logs - one.astype(F32)
    two = rest.astype(BF16)
    three = (rest - two.astype(F32)).astype(BF16)
    row = lax.broadcasted_iota(jnp.int32, (LOGS, logs.shape[1]), 0)
    ref[state:, :] = jnp.where(row == 0, one, jnp.where(row == 1, two, three))


def get_logs(ref, state):
    parts = ref[state:, :].astype(F32)
    return parts[0:1] + parts[1:2] + parts[2:3]


def states_kernel(
    heads, state, place, own_ref, c_ref, rate_ref, mine_ref, give_ref, early_ref, run_ref, turn_ref,
    xs, tail
):
    tokens = own_ref.shape[0]
    cols = early_ref.shape[1]
    width = cols // heads
    core, y = place[0], place[1]
    xs[core] = own_ref[...]
    xs[1 - core] = c_ref[...]
    i = lax.broadcasted_iota(jnp.int32, (tokens, tokens), 0)
    j = lax.broadcasted_iota(jnp.int32, (tokens, tokens), 1)
    lower_ones = (j <= i).astype(F32)
    upper_ones = (i <= j).astype(F32)
    low = lax.broadcasted_iota(jnp.int32, (1, 2 * width), 1) < width
    rates = rate_ref[...]
    shift = lax.rem(128 - core * heads, 128)
    kept = None
    offset = None
    for b in range(2):
        write = xs[b, :, cols : cols + state]
        high = xs[b, :, cols + 2 * state :].astype(F32)
        little = pltpu.roll(high, 64, 1)
        level = jnp.floor(high * 0.0625)
        lower = high * 64.0 + little - 1024.0 * level
        step = -rates * (1.0 + lower * (1.0 / 128.0)) - 0.125 * level
        step = jnp.where(j < heads, pltpu.roll(step, shift, 1), 0.0)
        run = jnp.dot(
            lower_ones, step, preferred_element_type=F32, precision=lax.Precision.HIGHEST
        )
        run_ref[b] = run
        turn_ref[b] = tn_dot(step, upper_ones, lax.Precision.HIGHEST)
        end = run[tokens - 1 : tokens, :]
        offset = end if b == 0 else offset + end
        to_end = jnp.exp(end - run)
        scaled = []
        for pair in range(heads // 2):
            tile = xs[b, :, pair * 2 * width : (pair + 1) * 2 * width]
            weight = jnp.where(
                low, to_end[:, 2 * pair : 2 * pair + 1], to_end[:, 2 * pair + 1 : 2 * pair + 2]
            )
            scaled.append((weight * tile.astype(F32)).astype(BF16))
        added = tn_dot(write, jnp.concatenate(scaled, axis=1))
        if b == 0:
            kept = added
            early_ref[...] = kept.astype(BF16)
        else:
            kept = spread(jnp.exp(end), heads // 2, width) * kept + added
    tail[0:state, :] = kept.astype(BF16)
    put_logs(tail, state, spread(offset, heads // 2, width))
    mine_ref[...] = tail[:, lanes(y, cols // 2)]
    give_ref[...] = tail[:, lanes(1 - y, cols // 2)]


def local_kernel(heads, state, place, xs, early_ref, run_ref, turn_ref, mixed_ref):
    tokens = run_ref.shape[1]
    cols = mixed_ref.shape[2]
    width = cols // heads
    i = lax.broadcasted_iota(jnp.int32, (tokens, tokens), 0)
    j = lax.broadcasted_iota(jnp.int32, (tokens, tokens), 1)
    low = lax.broadcasted_iota(jnp.int32, (1, 2 * width), 1) < width
    for b in range(2):
        write = xs[b, :, cols : cols + state]
        read = xs[b, :, cols + state : cols + 2 * state]
        run = run_ref[b]
        inner = jnp.where(j <= i, nt_dot(read, write), 0.0)
        if b > 0:
            fade = jnp.exp(run)
            seen = jnp.dot(read, early_ref[...], preferred_element_type=F32)
        for pair in range(heads // 2):
            part = slice(pair * 2 * width, (pair + 1) * 2 * width)
            tile = xs[b, :, part]
            mixes = []
            for h in (2 * pair, 2 * pair + 1):
                gap = jnp.minimum(run[:, h : h + 1] - turn_ref[b, h : h + 1, :], 0.0)
                mixes.append((inner * jnp.exp(gap)).astype(BF16))
            zero = jnp.zeros_like(tile)
            stacked = jnp.concatenate(
                [jnp.where(low, tile, zero), jnp.where(low, zero, tile)], axis=0
            )
            mixed = jnp.dot(jnp.concatenate(mixes, axis=1), stacked, preferred_element_type=F32)
            if b > 0:
                mixed = mixed + seen[:, part] * jnp.where(
                    low, fade[:, 2 * pair : 2 * pair + 1], fade[:, 2 * pair + 1 : 2 * pair + 2]
                )
            mixed_ref[b, :, part] = mixed


def pick(place, low_ref, high_ref, out_ref):
    @pl.when(place[1] == 0)
    def _():
        out_ref[...] = low_ref[...]

    @pl.when(place[1] != 0)
    def _():
        out_ref[...] = high_ref[...]


def row_kernel(state, place, tail_ref, y_ref, low_ref, high_ref, span_ref, first_ref, to_y):
    pick(place, low_ref, high_ref, to_y)
    first = place[1] == 0
    mine = tail_ref[0:state, :].astype(F32)
    theirs = y_ref[0:state, :].astype(F32)
    my_log = get_logs(tail_ref, state)
    their_log = get_logs(y_ref, state)
    later = jnp.where(first, theirs, mine)
    earlier = jnp.where(first, mine, theirs)
    decay = jnp.exp(jnp.where(first, their_log, my_log))
    span_ref[0:state, :] = (later + decay * earlier).astype(BF16)
    put_logs(span_ref, state, my_log + their_log)
    first_ref[...] = jnp.where(first, tail_ref[...].astype(F32), y_ref[...].astype(F32)).astype(BF16)


def join(state, old_ref, new, new_logs):
    if old_ref is None:
        return new, new_logs
    logs = get_logs(old_ref, state)
    return old_ref[0:state, :].astype(F32) + jnp.exp(logs) * new, logs + new_logs


def hop_kernel(state, distance, last, place, *refs):
    refs = list(refs)
    span_ref = refs.pop(0)
    before_ref = refs.pop(0) if distance > 1 else None
    new_ref = refs.pop(0)
    ok = place[2] >= distance
    new = jnp.where(ok, new_ref[0:state, :].astype(F32), 0.0)
    new_logs = jnp.where(ok, get_logs(new_ref, state), 0.0)
    before, before_logs = join(state, before_ref, new, new_logs)
    if last:
        first_ref, keep_ref, give_ref = refs
        second, _ = join(state, first_ref, before, before_logs)
        y = place[1]
        keep_ref[...] = jnp.where(y == 0, before, second).astype(BF16)
        give_ref[...] = jnp.where(y == 0, second, before).astype(BF16)
    else:
        span_out, before_out = refs
        span, span_logs = join(state, span_ref, new, new_logs)
        span_out[0:state, :] = span.astype(BF16)
        put_logs(span_out, state, span_logs)
        before_out[0:state, :] = before.astype(BF16)
        put_logs(before_out, state, before_logs)


def finish_kernel(
    heads, state, place, mixed_ref, run_ref, xs, mine_ref, other_ref, self_ref, c_ref
):
    core = place[0]
    y = place[1]
    cols = mixed_ref.shape[2]
    width = cols // heads
    mine = mine_ref[...]
    other = other_ref[...]
    entering = jnp.concatenate(
        [jnp.where(y == 0, mine, other), jnp.where(y == 0, other, mine)], axis=1
    )
    a = lax.broadcasted_iota(jnp.int32, (4 * width, 2 * width), 0)
    b = lax.broadcasted_iota(jnp.int32, (4 * width, 2 * width), 1)
    same = (lax.rem(a, 2 * width) < width) == (b < width)
    average = jnp.where(same, 1.0 / width, 0.0).astype(BF16)
    low = lax.broadcasted_iota(jnp.int32, (1, 2 * width), 1) < width
    for out_ref, at in ((c_ref, 1 - core), (self_ref, core)):
        read = xs[at, :, cols + state : cols + 2 * state]
        seen = jnp.dot(read, entering, preferred_element_type=F32)
        ahead = jnp.where(at == 0, 0.0, run_ref[0, run_ref.shape[1] - 1 :, :])
        fade = jnp.exp(run_ref[at] + ahead)
        for pair in range(heads // 2):
            part = slice(pair * 2 * width, (pair + 1) * 2 * width)
            tile = mixed_ref[at, :, part] + seen[:, part] * jnp.where(
                low, fade[:, 2 * pair : 2 * pair + 1], fade[:, 2 * pair + 1 : 2 * pair + 2]
            )
            square = tile * tile
            big = square.astype(BF16)
            small = (square - big.astype(F32)).astype(BF16)
            mean = jnp.dot(
                jnp.concatenate([big, small], axis=1), average, preferred_element_type=F32
            )
            out_ref[:, part] = (tile * lax.rsqrt(mean + 1e-05)).astype(BF16)


def collect_kernel(place, self_ref, c_ref, out_ref):
    core = place[0]
    cols = self_ref.shape[1]
    out_ref[:, lanes(core, cols)] = self_ref[...]
    out_ref[:, lanes(1 - core, cols)] = c_ref[...]


def after(value, *others):
    return lax.optimization_barrier((value, *others))[0]


def shards(
    ssm_inputs, state_write, state_read, decay_codes, decay_rate, queries, keys_values, segment_ids
):
    tokens, channels = ssm_inputs.shape
    heads = decay_rate.shape[0]
    state = state_write.shape[1]
    cols = channels // 2
    devices = lax.axis_size("seq")
    rows = devices // ROW
    send = lambda x, route: lax.ppermute(x, "seq", [(i, route(i)) for i in range(devices)])
    swap_c = lambda i: i ^ 1
    swap_y = lambda i: i ^ 2
    up = lambda n: lambda i: (i + n * ROW) % devices
    kv_width = keys_values.shape[2]
    half = cols // 2

    own, docs, mine, to_c, rates = call(
        pack_kernel,
        "pack",
        1.5,
        [
            ssm_inputs,
            state_write,
            state_read,
            decay_codes.T,
            keys_values,
            segment_ids[None, :],
            decay_rate[None, :],
        ],
        (
            shaped(2 * tokens + 16, kv_width),
            shaped(tokens, tokens, dtype=F32),
            shaped(tokens, cols + 2 * state + 128),
            shaped(tokens, cols + 2 * state + 128),
            shaped(1, 128, dtype=F32),
        ),
        [
            VMEM((heads, tokens), jnp.int32),
            VMEM((1, tokens), jnp.int32),
            VMEM((1, heads), F32),
            pltpu.SemaphoreType.DMA((11,)),
        ],
        True,
    )
    from_c = send(to_c, swap_c)
    behind2 = send(own, up(1))
    partner = send(own, swap_c)

    tail, tail_out, early, run, run_t, blocks = call(
        functools.partial(states_kernel, heads // 2, state),
        "states",
        2.0,
        [mine, from_c, rates],
        (
            shaped(state + LOGS, half),
            shaped(state + LOGS, half),
            shaped(state, cols),
            shaped(2, tokens, 128, dtype=F32),
            shaped(2, 128, tokens, dtype=F32),
            shaped(2, tokens, cols + 2 * state + 128),
        ),
        [VMEM((state + LOGS, cols), BF16)],
    )
    tail_y = send(tail_out, swap_y)
    carry = attend(
        after(queries, tail), docs, [own, partner], ((0, False), (0, True)), None, False
    )
    tail_y = after(tail_y, carry[0])
    span, first, to_y = call(
        functools.partial(row_kernel, state),
        "row",
        20.0,
        [tail, tail_y, own, behind2],
        (shaped(state + LOGS, half),) * 2 + (shaped(2 * tokens + 16, kv_width),),
    )
    new = send(span, up(1))
    behind2 = after(behind2, span)
    behind4 = send(behind2, up(1))
    behind1 = send(to_y, swap_y)
    behind2c = send(behind2, swap_c)
    mixed = call(
        functools.partial(local_kernel, heads // 2, state),
        "local",
        3.0,
        [after(blocks, span), early, run, run_t],
        shaped(2, tokens, cols, dtype=F32),
    )
    new = after(new, mixed)
    before = None
    distance = 1
    while distance < rows:
        last = 2 * distance >= rows
        out = call(
            functools.partial(hop_kernel, state, distance, last),
            "hop%d" % distance,
            20.0,
            [span] + [before] * (distance > 1) + [new] + [first] * last,
            (shaped(state, half) if last else shaped(state + LOGS, half),) * 2,
        )
        if last:
            keep, give = out
        else:
            span, before = out
            new = send(span, up(2 * distance))
        if distance == 1:
            carry = attend(
                after(queries, before),
                docs,
                [behind2, behind2c],
                ((2, False), (2, True)),
                carry,
                False,
            )
            behind4, behind1 = after(behind4, carry[0]), after(behind1, carry[0])
            behind1c = send(behind1, swap_c)
            behind4c = send(behind4, swap_c)
            to_y = call(
                pick,
                "pick",
                20.0,
                [behind2, behind4],
                shaped(2 * tokens + 16, kv_width),
            )
            behind3 = send(to_y, swap_y)
            new = after(new, to_y)
        distance *= 2
    carry = attend(
        after(queries, give),
        docs,
        [behind1, behind1c, behind4, behind4c],
        ((1, False), (1, True), (4, False), (4, True)),
        carry,
        False,
    )
    behind3 = after(behind3, carry[0])
    behind3c = send(behind3, swap_c)
    other_half = after(send(give, swap_y), carry[0])
    done, for_c = call(
        functools.partial(finish_kernel, heads // 2, state),
        "finish",
        1.7,
        [mixed, run, blocks, keep, other_half],
        (shaped(tokens, cols),) * 2,
    )
    back_c = send(for_c, swap_c)
    attn_output = attend(
        after(queries, for_c),
        docs,
        [behind3, behind3c],
        ((3, False), (3, True)),
        carry,
        True,
    )
    ssm_output = call(
        collect_kernel,
        "collect",
        0.8,
        [done, after(back_c, attn_output)],
        shaped(tokens, channels),
    )
    return (ssm_output, attn_output)


def solution(mesh):
    return jax.shard_map(
        shards,
        mesh=mesh,
        in_specs=(
            P(("groups", "seq"), None),
            P(("groups", "seq"), None),
            P(("groups", "seq"), None),
            P(("groups", "seq"), None),
            P(),
            P(None, ("groups", "seq"), None),
            P(None, ("groups", "seq"), None),
            P(("groups", "seq")),
        ),
        out_specs=(P(("groups", "seq"), None), P(None, ("groups", "seq"), None)),
        check_vma=False,
    )
```

```python
import functools
import math

import jax
import jax.numpy as jnp
from jax import lax
from jax.experimental import pallas as pl
from jax.experimental.pallas import tpu as pltpu
from jax.sharding import PartitionSpec as P

KV_HEADS = 4
HEAD = 128
ROW = 4
FAR = -1e30
SCALE = HEAD ** (-0.5) * math.log2(math.e)
F32 = jnp.float32
BF16 = jnp.bfloat16
VMEM = pltpu.VMEM
IN_VMEM = pl.BlockSpec(memory_space=pltpu.VMEM)
LOGS = 16


def nt_dot(a, b):
    return lax.dot_general(a, b, (((1,), (1,)), ((), ())), preferred_element_type=F32)


def tn_dot(a, b, precision=None):
    return lax.dot_general(
        a, b, (((0,), (0,)), ((), ())), preferred_element_type=F32, precision=precision
    )


def lanes(number, width):
    return pl.ds(pl.multiple_of(number * width, width), width)


def call(kernel, name, micros, args, outs, scratch=(), stay=False, mib=8, leaves=False):
    out_spec = pl.BlockSpec(memory_space=pltpu.HBM) if leaves else IN_VMEM
    spec = pl.BlockSpec(memory_space=pltpu.HBM) if stay else IN_VMEM

    def placed(*refs):
        rank = lax.axis_index("seq")
        kernel((rank & 1, (rank >> 1) & 1, rank >> 2, rank >> 1), *refs)

    return pl.pallas_call(
        placed,
        name=name,
        out_shape=outs,
        in_specs=[spec] * len(args),
        out_specs=jax.tree.map(lambda _: out_spec, outs),
        scratch_shapes=list(scratch),
        cost_estimate=pl.CostEstimate(
            flops=int(micros * 1.15e9), bytes_accessed=0, transcendentals=0
        ),
        compiler_params=pltpu.CompilerParams(vmem_limit_bytes=mib * 1024 * 1024),
    )(*[pltpu.with_memory_space_constraint(a, pltpu.HBM) if stay else a for a in args])


def shaped(*shape, dtype=BF16):
    return jax.ShapeDtypeStruct(shape, dtype)


def pack_kernel(
    place, x, write, read, codes, kv, seg, rate, own, docs, mine, to_c, rates, code_buf, seg_buf, rate_buf,
    sems
):
    core = place[0]
    tokens, state = write.shape
    heads = codes.shape[0]
    half = x.shape[1] // 2
    copies = [
        (kv.at[0], own.at[0:tokens]),
        (kv.at[1], own.at[tokens : 2 * tokens]),
        (x.at[:, lanes(1 - core, half)], to_c.at[:, 0:half]),
        (write, to_c.at[:, half : half + state]),
        (read, to_c.at[:, half + state : half + 2 * state]),
        (codes, code_buf),
        (seg, seg_buf),
        (rate, rate_buf),
        (x.at[:, lanes(core, half)], mine.at[:, 0:half]),
        (write, mine.at[:, half : half + state]),
        (read, mine.at[:, half + state : half + 2 * state]),
    ]
    copies = [
        pltpu.make_async_copy(source, target, sems.at[n])
        for n, (source, target) in enumerate(copies)
    ]
    for copy in copies:
        copy.start()
    own[2 * tokens :, tokens:] = jnp.zeros((16, own.shape[1] - tokens), BF16)
    for copy in copies:
        copy.wait()
    codes_of = (seg_buf[...] + 1).astype(F32).astype(BF16)
    own[2 * tokens :, 0:tokens] = jnp.broadcast_to(codes_of, (16, tokens))
    docs[...] = jnp.transpose(jnp.broadcast_to(codes_of.astype(F32), (tokens, tokens)))
    code = code_buf[...]
    high = (code >> 6).astype(F32)
    low = (code & 63).astype(F32)
    gap = jnp.zeros((64 - heads, tokens), F32)
    both = jnp.transpose(jnp.concatenate([high, gap, low, gap], axis=0)).astype(BF16)
    mine[:, half + 2 * state :] = both
    to_c[:, half + 2 * state :] = both
    rates[...] = jnp.concatenate([rate_buf[...], jnp.zeros((1, 128 - heads), F32)], axis=1)


def attend_kernel(kinds, first, last, place, q_ref, doc_ref, *refs):
    count = len(kinds)
    rows = q_ref.shape[1]
    pieces = refs[:count]
    at = count
    if not first:
        acc_in, peak_in, sum_in = refs[at : at + 3]
        at += 3
    if last:
        out_ref = refs[at]
        at += 1
    else:
        acc_out, peak_out, sum_out = refs[at : at + 3]
        at += 3
    bias = refs[at]
    core = place[0]
    chip = place[3]
    group = q_ref.shape[2] // HEAD // KV_HEADS
    if last:
        final_ref = out_ref
        out_ref, sems = refs[at + 1 :]

    def leave(head):
        cols = slice(head * group * HEAD, (head + 1) * group * HEAD)
        return pltpu.make_async_copy(
            out_ref.at[:, :, cols], final_ref.at[:, :, cols], sems.at[head]
        )

    def over_heads(body):
        for head in range(KV_HEADS):
            tiles = [
                (layer, slice((head * group + r) * HEAD, (head * group + r + 1) * HEAD))
                for layer in range(2)
                for r in range(group)
            ]
            body(head, [tiles[n : n + 2] for n in range(0, len(tiles), 2)])
            if last:
                leave(head).start()
        if last:
            for head in range(KV_HEADS):
                leave(head).wait()

    def stack(ref, pair):
        return jnp.concatenate([ref[layer, :, cols] for layer, cols in pair], axis=0)

    def unstack(ref, pair, value):
        for n, (layer, cols) in enumerate(pair):
            ref[layer, :, cols] = value[n * rows : (n + 1) * rows]

    def visit(here):
        mine = doc_ref[...]
        i = lax.broadcasted_iota(jnp.int32, (rows, rows), 0)
        j = lax.broadcasted_iota(jnp.int32, (rows, rows), 1)
        for n, (behind, other) in enumerate(kinds[:here]):
            theirs = pieces[n][2 * rows : 2 * rows + 16, 0:rows].astype(F32)[0:1]
            ok = theirs == mine
            if behind == 0 and not other:
                ok = ok & (j <= i)
            elif behind == 0:
                ok = ok & (j < rows * core)
            elif behind == 4 and not other:
                ok = ok & (j > i)
            elif behind == 4:
                ok = ok & (j < rows * (1 - core))
            bias[:, n * rows : (n + 1) * rows] = jnp.where(ok, 0.0, FAR)
        span = slice(0, here * rows)
        ones = jnp.ones((rows, HEAD), BF16)

        def body(head, pairs):
            cols = slice(head * HEAD, (head + 1) * HEAD)
            keys = jnp.concatenate([piece[0:rows, cols] for piece in pieces[:here]], axis=0)
            values = jnp.concatenate(
                [
                    jnp.concatenate([piece[rows : 2 * rows, cols], ones], axis=1)
                    for piece in pieces[:here]
                ],
                axis=0,
            )
            for pair in pairs:
                scores = nt_dot(stack(q_ref, pair), keys) * SCALE
                scores = scores + jnp.concatenate([bias[:, span]] * 2, axis=0)
                peak = jnp.max(scores, axis=1, keepdims=True)
                if first:
                    probs = jnp.exp2(scores - peak)
                else:
                    old = stack(peak_in, pair)
                    peak = jnp.maximum(old, peak)
                    fade = jnp.exp2(old - peak)
                    probs = jnp.concatenate(
                        [
                            jnp.exp2(scores[:, n * rows : (n + 1) * rows] - peak)
                            for n in range(here)
                        ],
                        axis=1,
                    )
                both = jnp.dot(probs.astype(BF16), values, preferred_element_type=F32)
                acc = both[:, :HEAD]
                total = both[:, HEAD:]
                if not first:
                    acc = acc + fade * stack(acc_in, pair)
                    total = total + fade * stack(sum_in, pair)
                if last:
                    unstack(out_ref, pair, (acc / total).astype(BF16))
                else:
                    unstack(acc_out, pair, acc)
                    unstack(sum_out, pair, total)
                    unstack(peak_out, pair, jnp.broadcast_to(peak, acc.shape))

        over_heads(body)

    def skip():
        def body(head, pairs):
            for pair in pairs:
                for layer, cols in pair:
                    out_ref[layer, :, cols] = (
                        acc_in[layer, :, cols] / sum_in[layer, :, cols]
                    ).astype(BF16)

        if last:
            over_heads(body)
        else:
            acc_out[...] = acc_in[...]
            sum_out[...] = sum_in[...]
            peak_out[...] = peak_in[...]

    steps = sorted({behind for behind, _ in kinds})
    for n, behind in enumerate(steps):
        here = sum(other <= behind for other, _ in kinds)
        enough = chip >= behind
        if n + 1 < len(steps):
            enough = enough & (chip < steps[n + 1])
        if behind == 0:
            visit(here)
        else:
            pl.when(enough)(functools.partial(visit, here))
    if not first:
        pl.when(chip < steps[0])(skip)


def attend(queries, docs, pieces, kinds, carry, last):
    layers, tokens, width = queries.shape
    count = len(kinds)
    partial = shaped(layers, tokens, width, dtype=F32)
    args = [queries, docs] + list(pieces) + list(carry or ())
    outs = shaped(layers, tokens, width) if last else (partial,) * 3
    return call(
        functools.partial(attend_kernel, kinds, carry is None, last),
        "attend%d" % kinds[-1][0],
        0.5 + 1.05 * count,
        args,
        outs,
        [
            VMEM((tokens, count * tokens), F32),
        ]
        + ([VMEM(queries.shape, BF16), pltpu.SemaphoreType.DMA((KV_HEADS,))] if last else []),
        mib=20,
        leaves=last,
    )


def spread(columns, pairs, width):
    low = lax.broadcasted_iota(jnp.int32, (1, 2 * width), 1) < width
    parts = [
        jnp.where(low, columns[:, 2 * k : 2 * k + 1], columns[:, 2 * k + 1 : 2 * k + 2])
        for k in range(pairs)
    ]
    return jnp.concatenate(parts, axis=1)


def put_logs(ref, state, logs):
    one = logs.astype(BF16)
    rest = logs - one.astype(F32)
    two = rest.astype(BF16)
    three = (rest - two.astype(F32)).astype(BF16)
    row = lax.broadcasted_iota(jnp.int32, (LOGS, logs.shape[1]), 0)
    ref[state:, :] = jnp.where(row == 0, one, jnp.where(row == 1, two, three))


def get_logs(ref, state):
    parts = ref[state:, :].astype(F32)
    return parts[0:1] + parts[1:2] + parts[2:3]


def states_kernel(
    heads, state, place, own_ref, c_ref, rate_ref, mine_ref, give_ref, early_ref, run_ref, turn_ref,
    xs, tail
):
    tokens = own_ref.shape[0]
    cols = early_ref.shape[1]
    width = cols // heads
    core, y = place[0], place[1]
    xs[core] = own_ref[...]
    xs[1 - core] = c_ref[...]
    i = lax.broadcasted_iota(jnp.int32, (tokens, tokens), 0)
    j = lax.broadcasted_iota(jnp.int32, (tokens, tokens), 1)
    lower_ones = (j <= i).astype(F32)
    upper_ones = (i <= j).astype(F32)
    low = lax.broadcasted_iota(jnp.int32, (1, 2 * width), 1) < width
    rates = rate_ref[...]
    shift = lax.rem(128 - core * heads, 128)
    kept = None
    offset = None
    for b in range(2):
        write = xs[b, :, cols : cols + state]
        high = xs[b, :, cols + 2 * state :].astype(F32)
        little = pltpu.roll(high, 64, 1)
        level = jnp.floor(high * 0.0625)
        lower = high * 64.0 + little - 1024.0 * level
        step = -rates * (1.0 + lower * (1.0 / 128.0)) - 0.125 * level
        step = jnp.where(j < heads, pltpu.roll(step, shift, 1), 0.0)
        run = jnp.dot(
            lower_ones, step, preferred_element_type=F32, precision=lax.Precision.HIGHEST
        )
        run_ref[b] = run
        turn_ref[b] = tn_dot(step, upper_ones, lax.Precision.HIGHEST)
        end = run[tokens - 1 : tokens, :]
        offset = end if b == 0 else offset + end
        to_end = jnp.exp(end - run)
        scaled = []
        for pair in range(heads // 2):
            tile = xs[b, :, pair * 2 * width : (pair + 1) * 2 * width]
            weight = jnp.where(
                low, to_end[:, 2 * pair : 2 * pair + 1], to_end[:, 2 * pair + 1 : 2 * pair + 2]
            )
            scaled.append((weight * tile.astype(F32)).astype(BF16))
        added = tn_dot(write, jnp.concatenate(scaled, axis=1))
        if b == 0:
            kept = added
            early_ref[...] = kept.astype(BF16)
        else:
            kept = spread(jnp.exp(end), heads // 2, width) * kept + added
    tail[0:state, :] = kept.astype(BF16)
    put_logs(tail, state, spread(offset, heads // 2, width))
    mine_ref[...] = tail[:, lanes(y, cols // 2)]
    give_ref[...] = tail[:, lanes(1 - y, cols // 2)]


def local_kernel(heads, state, place, xs, early_ref, run_ref, turn_ref, mixed_ref):
    tokens = run_ref.shape[1]
    cols = mixed_ref.shape[2]
    width = cols // heads
    i = lax.broadcasted_iota(jnp.int32, (tokens, tokens), 0)
    j = lax.broadcasted_iota(jnp.int32, (tokens, tokens), 1)
    low = lax.broadcasted_iota(jnp.int32, (1, 2 * width), 1) < width
    for b in range(2):
        write = xs[b, :, cols : cols + state]
        read = xs[b, :, cols + state : cols + 2 * state]
        run = run_ref[b]
        inner = jnp.where(j <= i, nt_dot(read, write), 0.0)
        if b > 0:
            fade = jnp.exp(run)
            seen = jnp.dot(read, early_ref[...], preferred_element_type=F32)
        for pair in range(heads // 2):
            part = slice(pair * 2 * width, (pair + 1) * 2 * width)
            tile = xs[b, :, part]
            mixes = []
            for h in (2 * pair, 2 * pair + 1):
                gap = jnp.minimum(run[:, h : h + 1] - turn_ref[b, h : h + 1, :], 0.0)
                mixes.append((inner * jnp.exp(gap)).astype(BF16))
            zero = jnp.zeros_like(tile)
            stacked = jnp.concatenate(
                [jnp.where(low, tile, zero), jnp.where(low, zero, tile)], axis=0
            )
            mixed = jnp.dot(jnp.concatenate(mixes, axis=1), stacked, preferred_element_type=F32)
            if b > 0:
                mixed = mixed + seen[:, part] * jnp.where(
                    low, fade[:, 2 * pair : 2 * pair + 1], fade[:, 2 * pair + 1 : 2 * pair + 2]
                )
            mixed_ref[b, :, part] = mixed


def pick(place, low_ref, high_ref, out_ref):
    @pl.when(place[1] == 0)
    def _():
        out_ref[...] = low_ref[...]

    @pl.when(place[1] != 0)
    def _():
        out_ref[...] = high_ref[...]


def row_kernel(state, place, tail_ref, y_ref, span_ref, first_ref):
    first = place[1] == 0
    mine = tail_ref[0:state, :].astype(F32)
    theirs = y_ref[0:state, :].astype(F32)
    my_log = get_logs(tail_ref, state)
    their_log = get_logs(y_ref, state)
    later = jnp.where(first, theirs, mine)
    earlier = jnp.where(first, mine, theirs)
    decay = jnp.exp(jnp.where(first, their_log, my_log))
    span_ref[0:state, :] = (later + decay * earlier).astype(BF16)
    put_logs(span_ref, state, my_log + their_log)
    first_ref[...] = jnp.where(first, tail_ref[...].astype(F32), y_ref[...].astype(F32)).astype(BF16)


def join(state, old_ref, new, new_logs):
    if old_ref is None:
        return new, new_logs
    logs = get_logs(old_ref, state)
    return old_ref[0:state, :].astype(F32) + jnp.exp(logs) * new, logs + new_logs


def hop_kernel(state, distance, last, place, *refs):
    refs = list(refs)
    span_ref = refs.pop(0)
    before_ref = refs.pop(0) if distance > 1 else None
    new_ref = refs.pop(0)
    ok = place[2] >= distance
    new = jnp.where(ok, new_ref[0:state, :].astype(F32), 0.0)
    new_logs = jnp.where(ok, get_logs(new_ref, state), 0.0)
    before, before_logs = join(state, before_ref, new, new_logs)
    if last:
        first_ref, keep_ref, give_ref = refs
        second, _ = join(state, first_ref, before, before_logs)
        y = place[1]
        keep_ref[...] = jnp.where(y == 0, before, second).astype(BF16)
        give_ref[...] = jnp.where(y == 0, second, before).astype(BF16)
    else:
        span_out, before_out = refs
        span, span_logs = join(state, span_ref, new, new_logs)
        span_out[0:state, :] = span.astype(BF16)
        put_logs(span_out, state, span_logs)
        before_out[0:state, :] = before.astype(BF16)
        put_logs(before_out, state, before_logs)


def finish_kernel(
    heads, state, place, mixed_ref, run_ref, xs, mine_ref, other_ref, self_ref, c_ref
):
    core = place[0]
    y = place[1]
    cols = mixed_ref.shape[2]
    width = cols // heads
    mine = mine_ref[...]
    other = other_ref[...]
    entering = jnp.concatenate(
        [jnp.where(y == 0, mine, other), jnp.where(y == 0, other, mine)], axis=1
    )
    a = lax.broadcasted_iota(jnp.int32, (4 * width, 2 * width), 0)
    b = lax.broadcasted_iota(jnp.int32, (4 * width, 2 * width), 1)
    same = (lax.rem(a, 2 * width) < width) == (b < width)
    average = jnp.where(same, 1.0 / width, 0.0).astype(BF16)
    low = lax.broadcasted_iota(jnp.int32, (1, 2 * width), 1) < width
    for out_ref, at in ((c_ref, 1 - core), (self_ref, core)):
        read = xs[at, :, cols + state : cols + 2 * state]
        seen = jnp.dot(read, entering, preferred_element_type=F32)
        ahead = jnp.where(at == 0, 0.0, run_ref[0, run_ref.shape[1] - 1 :, :])
        fade = jnp.exp(run_ref[at] + ahead)
        for pair in range(heads // 2):
            part = slice(pair * 2 * width, (pair + 1) * 2 * width)
            tile = mixed_ref[at, :, part] + seen[:, part] * jnp.where(
                low, fade[:, 2 * pair : 2 * pair + 1], fade[:, 2 * pair + 1 : 2 * pair + 2]
            )
            square = tile * tile
            big = square.astype(BF16)
            small = (square - big.astype(F32)).astype(BF16)
            mean = jnp.dot(
                jnp.concatenate([big, small], axis=1), average, preferred_element_type=F32
            )
            out_ref[:, part] = (tile * lax.rsqrt(mean + 1e-05)).astype(BF16)


def collect_kernel(place, self_ref, c_ref, out_ref):
    core = place[0]
    cols = self_ref.shape[1]
    out_ref[:, lanes(core, cols)] = self_ref[...]
    out_ref[:, lanes(1 - core, cols)] = c_ref[...]


def after(value, *others):
    return lax.optimization_barrier((value, *others))[0]


def shards(
    ssm_inputs, state_write, state_read, decay_codes, decay_rate, queries, keys_values, segment_ids
):
    tokens, channels = ssm_inputs.shape
    heads = decay_rate.shape[0]
    state = state_write.shape[1]
    cols = channels // 2
    devices = lax.axis_size("seq")
    rows = devices // ROW
    send = lambda x, route: lax.ppermute(x, "seq", [(i, route(i)) for i in range(devices)])
    swap_c = lambda i: i ^ 1
    swap_y = lambda i: i ^ 2
    up = lambda n: lambda i: (i + n * ROW) % devices
    climb = lambda x, n=1: lax.ppermute(
        x, "seq", [(i, i + n * ROW) for i in range(devices - n * ROW)]
    )
    kv_width = keys_values.shape[2]
    half = cols // 2

    own, docs, mine, to_c, rates = call(
        pack_kernel,
        "pack",
        1.5,
        [
            ssm_inputs,
            state_write,
            state_read,
            decay_codes.T,
            keys_values,
            segment_ids[None, :],
            decay_rate[None, :],
        ],
        (
            shaped(2 * tokens + 16, kv_width),
            shaped(tokens, tokens, dtype=F32),
            shaped(tokens, cols + 2 * state + 128),
            shaped(tokens, cols + 2 * state + 128),
            shaped(1, 128, dtype=F32),
        ),
        [
            VMEM((heads, tokens), jnp.int32),
            VMEM((1, tokens), jnp.int32),
            VMEM((1, heads), F32),
            pltpu.SemaphoreType.DMA((11,)),
        ],
        True,
    )
    from_c = send(to_c, swap_c)
    behind2 = send(own, up(1))
    partner = send(own, swap_c)

    tail, tail_out, early, run, run_t, blocks = call(
        functools.partial(states_kernel, heads // 2, state),
        "states",
        2.0,
        [mine, from_c, rates],
        (
            shaped(state + LOGS, half),
            shaped(state + LOGS, half),
            shaped(state, cols),
            shaped(2, tokens, 128, dtype=F32),
            shaped(2, 128, tokens, dtype=F32),
            shaped(2, tokens, cols + 2 * state + 128),
        ),
        [VMEM((state + LOGS, cols), BF16)],
    )
    tail_y = send(tail_out, swap_y)
    carry = attend(
        after(queries, tail), docs, [own, partner], ((0, False), (0, True)), None, False
    )
    tail_y = after(tail_y, carry[1])
    span, first = call(
        functools.partial(row_kernel, state),
        "row",
        20.0,
        [tail, tail_y],
        (shaped(state + LOGS, half),) * 2,
    )
    new = send(span, up(1))
    behind2 = after(behind2, span)
    to_y = call(pick, "pick", 20.0, [own, behind2], shaped(2 * tokens + 16, kv_width))
    behind1 = send(to_y, swap_y)
    behind4 = send(after(behind2, to_y), up(1))
    behind2c = send(behind2, swap_c)
    mixed = call(
        functools.partial(local_kernel, heads // 2, state),
        "local",
        3.0,
        [after(blocks, to_y), early, run, run_t],
        shaped(2, tokens, cols, dtype=F32),
    )
    new = after(new, mixed)
    before = None
    distance = 1
    while distance < rows:
        last = 2 * distance >= rows
        out = call(
            functools.partial(hop_kernel, state, distance, last),
            "hop%d" % distance,
            20.0,
            [span] + [before] * (distance > 1) + [new] + [first] * last,
            (shaped(state, half) if last else shaped(state + LOGS, half),) * 2,
        )
        if last:
            keep, give = out
        else:
            span, before = out
            new = climb(span, 2 * distance)
        if distance == 1:
            carry = attend(
                after(queries, before),
                docs,
                [behind2, behind2c],
                ((2, False), (2, True)),
                carry,
                False,
            )
            behind4, behind1 = after(behind4, carry[1]), after(behind1, carry[1])
            behind1c = send(behind1, swap_c)
            behind3 = climb(behind1)
            behind4c = send(behind4, swap_c)
            new = after(new, carry[1])
        distance *= 2
    carry = attend(
        after(queries, give),
        docs,
        [behind1, behind1c, behind4, behind4c],
        ((1, False), (1, True), (4, False), (4, True)),
        carry,
        False,
    )
    behind3 = after(behind3, carry[1])
    behind3c = send(behind3, swap_c)
    other_half = after(send(give, swap_y), carry[1])
    done, for_c = call(
        functools.partial(finish_kernel, heads // 2, state),
        "finish",
        1.7,
        [mixed, run, blocks, keep, other_half],
        (shaped(tokens, cols),) * 2,
    )
    back_c = send(for_c, swap_c)
    attn_output = attend(
        after(queries, for_c),
        docs,
        [behind3, behind3c],
        ((3, False), (3, True)),
        carry,
        True,
    )
    ssm_output = call(
        collect_kernel,
        "collect",
        0.8,
        [done, after(back_c, attn_output)],
        shaped(tokens, channels),
    )
    return (ssm_output, attn_output)


def solution(mesh):
    return jax.shard_map(
        shards,
        mesh=mesh,
        in_specs=(
            P(("groups", "seq"), None),
            P(("groups", "seq"), None),
            P(("groups", "seq"), None),
            P(("groups", "seq"), None),
            P(),
            P(None, ("groups", "seq"), None),
            P(None, ("groups", "seq"), None),
            P(("groups", "seq")),
        ),
        out_specs=(P(("groups", "seq"), None), P(None, ("groups", "seq"), None)),
        check_vma=False,
    )
```

```python
import functools
import math

import jax
import jax.numpy as jnp
from jax import lax
from jax.experimental import pallas as pl
from jax.experimental.pallas import tpu as pltpu
from jax.sharding import PartitionSpec as P

KV_HEADS = 4
HEAD = 128
ROW = 4
FAR = -1e30
SCALE = HEAD ** (-0.5) * math.log2(math.e)
F32 = jnp.float32
BF16 = jnp.bfloat16
VMEM = pltpu.VMEM
IN_VMEM = pl.BlockSpec(memory_space=pltpu.VMEM)
LOGS = 16


def nt_dot(a, b):
    return lax.dot_general(a, b, (((1,), (1,)), ((), ())), preferred_element_type=F32)


def tn_dot(a, b, precision=None):
    return lax.dot_general(
        a, b, (((0,), (0,)), ((), ())), preferred_element_type=F32, precision=precision
    )


def lanes(number, width):
    return pl.ds(pl.multiple_of(number * width, width), width)


def call(kernel, name, micros, args, outs, scratch=(), stay=False, mib=8, leaves=False):
    out_spec = pl.BlockSpec(memory_space=pltpu.HBM) if leaves else IN_VMEM
    spec = pl.BlockSpec(memory_space=pltpu.HBM) if stay else IN_VMEM

    def placed(*refs):
        rank = lax.axis_index("seq")
        kernel((rank & 1, (rank >> 1) & 1, rank >> 2, rank >> 1), *refs)

    return pl.pallas_call(
        placed,
        name=name,
        out_shape=outs,
        in_specs=[spec] * len(args),
        out_specs=jax.tree.map(lambda _: out_spec, outs),
        scratch_shapes=list(scratch),
        cost_estimate=pl.CostEstimate(
            flops=int(micros * 1.15e9), bytes_accessed=0, transcendentals=0
        ),
        compiler_params=pltpu.CompilerParams(vmem_limit_bytes=mib * 1024 * 1024),
    )(*[pltpu.with_memory_space_constraint(a, pltpu.HBM) if stay else a for a in args])


def shaped(*shape, dtype=BF16):
    return jax.ShapeDtypeStruct(shape, dtype)


def pack_kernel(
    place, x, write, read, codes, kv, seg, rate, own, docs, mine, to_c, rates, code_buf, seg_buf, rate_buf,
    sems
):
    core = place[0]
    tokens, state = write.shape
    heads = codes.shape[0]
    half = x.shape[1] // 2
    copies = [
        (kv.at[0], own.at[0:tokens]),
        (kv.at[1], own.at[tokens : 2 * tokens]),
        (x.at[:, lanes(1 - core, half)], to_c.at[:, 0:half]),
        (write, to_c.at[:, half : half + state]),
        (read, to_c.at[:, half + state : half + 2 * state]),
        (codes, code_buf),
        (seg, seg_buf),
        (rate, rate_buf),
        (x.at[:, lanes(core, half)], mine.at[:, 0:half]),
        (write, mine.at[:, half : half + state]),
        (read, mine.at[:, half + state : half + 2 * state]),
    ]
    copies = [
        pltpu.make_async_copy(source, target, sems.at[n])
        for n, (source, target) in enumerate(copies)
    ]
    for copy in copies:
        copy.start()
    own[2 * tokens :, tokens:] = jnp.zeros((16, own.shape[1] - tokens), BF16)
    for copy in copies:
        copy.wait()
    codes_of = (seg_buf[...] + 1).astype(F32).astype(BF16)
    own[2 * tokens :, 0:tokens] = jnp.broadcast_to(codes_of, (16, tokens))
    docs[...] = jnp.transpose(jnp.broadcast_to(codes_of.astype(F32), (tokens, tokens)))
    code = code_buf[...]
    high = (code >> 6).astype(F32)
    low = (code & 63).astype(F32)
    gap = jnp.zeros((64 - heads, tokens), F32)
    both = jnp.transpose(jnp.concatenate([high, gap, low, gap], axis=0)).astype(BF16)
    mine[:, half + 2 * state :] = both
    to_c[:, half + 2 * state :] = both
    rates[...] = jnp.concatenate([rate_buf[...], jnp.zeros((1, 128 - heads), F32)], axis=1)


def attend_kernel(kinds, first, last, place, q_ref, doc_ref, *refs):
    count = len(kinds)
    rows = q_ref.shape[1]
    pieces = refs[:count]
    at = count
    if not first:
        acc_in, peak_in, sum_in = refs[at : at + 3]
        at += 3
    if last:
        out_ref = refs[at]
        at += 1
    else:
        acc_out, peak_out, sum_out = refs[at : at + 3]
        at += 3
    bias = refs[at]
    core = place[0]
    chip = place[3]
    group = q_ref.shape[2] // HEAD // KV_HEADS
    if last:
        final_ref = out_ref
        out_ref, sems = refs[at + 1 :]

    def leave(head):
        cols = slice(head * group * HEAD, (head + 1) * group * HEAD)
        return pltpu.make_async_copy(
            out_ref.at[:, :, cols], final_ref.at[:, :, cols], sems.at[head]
        )

    def over_heads(body):
        for head in range(KV_HEADS):
            tiles = [
                (layer, slice((head * group + r) * HEAD, (head * group + r + 1) * HEAD))
                for layer in range(2)
                for r in range(group)
            ]
            body(head, [tiles[n : n + 2] for n in range(0, len(tiles), 2)])
            if last:
                leave(head).start()
        if last:
            for head in range(KV_HEADS):
                leave(head).wait()

    def stack(ref, pair):
        return jnp.concatenate([ref[layer, :, cols] for layer, cols in pair], axis=0)

    def unstack(ref, pair, value):
        for n, (layer, cols) in enumerate(pair):
            ref[layer, :, cols] = value[n * rows : (n + 1) * rows]

    def visit(here):
        mine = doc_ref[...]
        i = lax.broadcasted_iota(jnp.int32, (rows, rows), 0)
        j = lax.broadcasted_iota(jnp.int32, (rows, rows), 1)
        for n, (behind, other) in enumerate(kinds[:here]):
            theirs = pieces[n][2 * rows : 2 * rows + 16, 0:rows].astype(F32)[0:1]
            ok = theirs == mine
            if behind == 0 and not other:
                ok = ok & (j <= i)
            elif behind == 0:
                ok = ok & (j < rows * core)
            elif behind == 4 and not other:
                ok = ok & (j > i)
            elif behind == 4:
                ok = ok & (j < rows * (1 - core))
            bias[:, n * rows : (n + 1) * rows] = jnp.where(ok, 0.0, FAR)
        span = slice(0, here * rows)
        ones = jnp.ones((rows, HEAD), BF16)

        def body(head, pairs):
            cols = slice(head * HEAD, (head + 1) * HEAD)
            keys = jnp.concatenate([piece[0:rows, cols] for piece in pieces[:here]], axis=0)
            values = jnp.concatenate(
                [
                    jnp.concatenate([piece[rows : 2 * rows, cols], ones], axis=1)
                    for piece in pieces[:here]
                ],
                axis=0,
            )
            for pair in pairs:
                scores = nt_dot(stack(q_ref, pair), keys) * SCALE
                scores = scores + jnp.concatenate([bias[:, span]] * 2, axis=0)
                peak = jnp.max(scores, axis=1, keepdims=True)
                if first:
                    probs = jnp.exp2(scores - peak)
                else:
                    old = stack(peak_in, pair)
                    peak = jnp.maximum(old, peak)
                    fade = jnp.exp2(old - peak)
                    probs = jnp.concatenate(
                        [
                            jnp.exp2(scores[:, n * rows : (n + 1) * rows] - peak)
                            for n in range(here)
                        ],
                        axis=1,
                    )
                both = jnp.dot(probs.astype(BF16), values, preferred_element_type=F32)
                acc = both[:, :HEAD]
                total = both[:, HEAD:]
                if not first:
                    acc = acc + fade * stack(acc_in, pair)
                    total = total + fade * stack(sum_in, pair)
                if last:
                    unstack(out_ref, pair, (acc / total).astype(BF16))
                else:
                    unstack(acc_out, pair, acc)
                    unstack(sum_out, pair, total)
                    unstack(peak_out, pair, jnp.broadcast_to(peak, acc.shape))

        over_heads(body)

    def skip():
        def body(head, pairs):
            for pair in pairs:
                for layer, cols in pair:
                    out_ref[layer, :, cols] = (
                        acc_in[layer, :, cols] / sum_in[layer, :, cols]
                    ).astype(BF16)

        if last:
            over_heads(body)
        else:
            acc_out[...] = acc_in[...]
            sum_out[...] = sum_in[...]
            peak_out[...] = peak_in[...]

    steps = sorted({behind for behind, _ in kinds})
    for n, behind in enumerate(steps):
        here = sum(other <= behind for other, _ in kinds)
        enough = chip >= behind
        if n + 1 < len(steps):
            enough = enough & (chip < steps[n + 1])
        if behind == 0:
            visit(here)
        else:
            pl.when(enough)(functools.partial(visit, here))
    if not first:
        pl.when(chip < steps[0])(skip)


def attend(queries, docs, pieces, kinds, carry, last):
    layers, tokens, width = queries.shape
    count = len(kinds)
    partial = shaped(layers, tokens, width, dtype=F32)
    args = [queries, docs] + list(pieces) + list(carry or ())
    outs = shaped(layers, tokens, width) if last else (partial,) * 3
    return call(
        functools.partial(attend_kernel, kinds, carry is None, last),
        "attend%d" % kinds[-1][0],
        0.5 + 1.05 * count,
        args,
        outs,
        [
            VMEM((tokens, count * tokens), F32),
        ]
        + ([VMEM(queries.shape, BF16), pltpu.SemaphoreType.DMA((KV_HEADS,))] if last else []),
        mib=20,
        leaves=last,
    )


def spread(columns, pairs, width):
    low = lax.broadcasted_iota(jnp.int32, (1, 2 * width), 1) < width
    parts = [
        jnp.where(low, columns[:, 2 * k : 2 * k + 1], columns[:, 2 * k + 1 : 2 * k + 2])
        for k in range(pairs)
    ]
    return jnp.concatenate(parts, axis=1)


def put_logs(ref, state, logs):
    one = logs.astype(BF16)
    rest = logs - one.astype(F32)
    two = rest.astype(BF16)
    three = (rest - two.astype(F32)).astype(BF16)
    row = lax.broadcasted_iota(jnp.int32, (LOGS, logs.shape[1]), 0)
    ref[state:, :] = jnp.where(row == 0, one, jnp.where(row == 1, two, three))


def get_logs(ref, state):
    parts = ref[state:, :].astype(F32)
    return parts[0:1] + parts[1:2] + parts[2:3]


def states_kernel(
    heads, state, place, own_ref, c_ref, rate_ref, mine_ref, give_ref, early_ref, run_ref, turn_ref,
    xs, tail
):
    tokens = own_ref.shape[0]
    cols = early_ref.shape[1]
    width = cols // heads
    core, y = place[0], place[1]
    xs[core] = own_ref[...]
    xs[1 - core] = c_ref[...]
    i = lax.broadcasted_iota(jnp.int32, (tokens, tokens), 0)
    j = lax.broadcasted_iota(jnp.int32, (tokens, tokens), 1)
    lower_ones = (j <= i).astype(F32)
    upper_ones = (i <= j).astype(F32)
    low = lax.broadcasted_iota(jnp.int32, (1, 2 * width), 1) < width
    rates = rate_ref[...]
    shift = lax.rem(128 - core * heads, 128)
    kept = None
    offset = None
    for b in range(2):
        write = xs[b, :, cols : cols + state]
        high = xs[b, :, cols + 2 * state :].astype(F32)
        little = pltpu.roll(high, 64, 1)
        level = jnp.floor(high * 0.0625)
        lower = high * 64.0 + little - 1024.0 * level
        step = -rates * (1.0 + lower * (1.0 / 128.0)) - 0.125 * level
        step = jnp.where(j < heads, pltpu.roll(step, shift, 1), 0.0)
        run = jnp.dot(
            lower_ones, step, preferred_element_type=F32, precision=lax.Precision.HIGHEST
        )
        run_ref[b] = run
        turn_ref[b] = tn_dot(step, upper_ones, lax.Precision.HIGHEST)
        end = run[tokens - 1 : tokens, :]
        offset = end if b == 0 else offset + end
        to_end = jnp.exp(end - run)
        scaled = []
        for pair in range(heads // 2):
            tile = xs[b, :, pair * 2 * width : (pair + 1) * 2 * width]
            weight = jnp.where(
                low, to_end[:, 2 * pair : 2 * pair + 1], to_end[:, 2 * pair + 1 : 2 * pair + 2]
            )
            scaled.append((weight * tile.astype(F32)).astype(BF16))
        added = tn_dot(write, jnp.concatenate(scaled, axis=1))
        if b == 0:
            kept = added
            early_ref[...] = kept.astype(BF16)
        else:
            kept = spread(jnp.exp(end), heads // 2, width) * kept + added
    tail[0:state, :] = kept.astype(BF16)
    put_logs(tail, state, spread(offset, heads // 2, width))
    mine_ref[...] = tail[:, lanes(y, cols // 2)]
    give_ref[...] = tail[:, lanes(1 - y, cols // 2)]


def local_kernel(heads, state, place, xs, early_ref, run_ref, turn_ref, mixed_ref):
    tokens = run_ref.shape[1]
    cols = mixed_ref.shape[2]
    width = cols // heads
    i = lax.broadcasted_iota(jnp.int32, (tokens, tokens), 0)
    j = lax.broadcasted_iota(jnp.int32, (tokens, tokens), 1)
    low = lax.broadcasted_iota(jnp.int32, (1, 2 * width), 1) < width
    for b in range(2):
        write = xs[b, :, cols : cols + state]
        read = xs[b, :, cols + state : cols + 2 * state]
        run = run_ref[b]
        inner = jnp.where(j <= i, nt_dot(read, write), 0.0)
        if b > 0:
            fade = jnp.exp(run)
            seen = jnp.dot(read, early_ref[...], preferred_element_type=F32)
        for pair in range(heads // 2):
            part = slice(pair * 2 * width, (pair + 1) * 2 * width)
            tile = xs[b, :, part]
            mixes = []
            for h in (2 * pair, 2 * pair + 1):
                gap = jnp.minimum(run[:, h : h + 1] - turn_ref[b, h : h + 1, :], 0.0)
                mixes.append((inner * jnp.exp(gap)).astype(BF16))
            zero = jnp.zeros_like(tile)
            stacked = jnp.concatenate(
                [jnp.where(low, tile, zero), jnp.where(low, zero, tile)], axis=0
            )
            mixed = jnp.dot(jnp.concatenate(mixes, axis=1), stacked, preferred_element_type=F32)
            if b > 0:
                mixed = mixed + seen[:, part] * jnp.where(
                    low, fade[:, 2 * pair : 2 * pair + 1], fade[:, 2 * pair + 1 : 2 * pair + 2]
                )
            mixed_ref[b, :, part] = mixed


def pick(place, low_ref, high_ref, out_ref):
    @pl.when(place[1] == 0)
    def _():
        out_ref[...] = low_ref[...]

    @pl.when(place[1] != 0)
    def _():
        out_ref[...] = high_ref[...]


def row_kernel(state, place, tail_ref, y_ref, span_ref, first_ref):
    first = place[1] == 0
    mine = tail_ref[0:state, :].astype(F32)
    theirs = y_ref[0:state, :].astype(F32)
    my_log = get_logs(tail_ref, state)
    their_log = get_logs(y_ref, state)
    later = jnp.where(first, theirs, mine)
    earlier = jnp.where(first, mine, theirs)
    decay = jnp.exp(jnp.where(first, their_log, my_log))
    span_ref[0:state, :] = (later + decay * earlier).astype(BF16)
    put_logs(span_ref, state, my_log + their_log)
    first_ref[...] = jnp.where(first, tail_ref[...].astype(F32), y_ref[...].astype(F32)).astype(BF16)


def join(state, old_ref, new, new_logs):
    if old_ref is None:
        return new, new_logs
    logs = get_logs(old_ref, state)
    return old_ref[0:state, :].astype(F32) + jnp.exp(logs) * new, logs + new_logs


def hop_kernel(state, distance, last, place, *refs):
    refs = list(refs)
    span_ref = refs.pop(0)
    before_ref = refs.pop(0) if distance > 1 else None
    new_ref = refs.pop(0)
    ok = place[2] >= distance
    new = jnp.where(ok, new_ref[0:state, :].astype(F32), 0.0)
    new_logs = jnp.where(ok, get_logs(new_ref, state), 0.0)
    before, before_logs = join(state, before_ref, new, new_logs)
    if last:
        first_ref, keep_ref, give_ref = refs
        second, _ = join(state, first_ref, before, before_logs)
        y = place[1]
        keep_ref[...] = jnp.where(y == 0, before, second).astype(BF16)
        give_ref[...] = jnp.where(y == 0, second, before).astype(BF16)
    else:
        span_out, before_out = refs
        span, span_logs = join(state, span_ref, new, new_logs)
        span_out[0:state, :] = span.astype(BF16)
        put_logs(span_out, state, span_logs)
        before_out[0:state, :] = before.astype(BF16)
        put_logs(before_out, state, before_logs)


def finish_kernel(
    heads, state, place, mixed_ref, run_ref, xs, mine_ref, other_ref, self_ref, c_ref
):
    core = place[0]
    y = place[1]
    cols = mixed_ref.shape[2]
    width = cols // heads
    mine = mine_ref[...]
    other = other_ref[...]
    entering = jnp.concatenate(
        [jnp.where(y == 0, mine, other), jnp.where(y == 0, other, mine)], axis=1
    )
    a = lax.broadcasted_iota(jnp.int32, (4 * width, 2 * width), 0)
    b = lax.broadcasted_iota(jnp.int32, (4 * width, 2 * width), 1)
    same = (lax.rem(a, 2 * width) < width) == (b < width)
    average = jnp.where(same, 1.0 / width, 0.0).astype(BF16)
    low = lax.broadcasted_iota(jnp.int32, (1, 2 * width), 1) < width
    for out_ref, at in ((c_ref, 1 - core), (self_ref, core)):
        read = xs[at, :, cols + state : cols + 2 * state]
        seen = jnp.dot(read, entering, preferred_element_type=F32)
        ahead = jnp.where(at == 0, 0.0, run_ref[0, run_ref.shape[1] - 1 :, :])
        fade = jnp.exp(run_ref[at] + ahead)
        for pair in range(heads // 2):
            part = slice(pair * 2 * width, (pair + 1) * 2 * width)
            tile = mixed_ref[at, :, part] + seen[:, part] * jnp.where(
                low, fade[:, 2 * pair : 2 * pair + 1], fade[:, 2 * pair + 1 : 2 * pair + 2]
            )
            square = tile * tile
            big = square.astype(BF16)
            small = (square - big.astype(F32)).astype(BF16)
            mean = jnp.dot(
                jnp.concatenate([big, small], axis=1), average, preferred_element_type=F32
            )
            out_ref[:, part] = (tile * lax.rsqrt(mean + 1e-05)).astype(BF16)


def collect_kernel(place, self_ref, c_ref, out_ref):
    core = place[0]
    cols = self_ref.shape[1]
    out_ref[:, lanes(core, cols)] = self_ref[...]
    out_ref[:, lanes(1 - core, cols)] = c_ref[...]


def after(value, *others):
    return lax.optimization_barrier((value, *others))[0]


def shards(
    ssm_inputs, state_write, state_read, decay_codes, decay_rate, queries, keys_values, segment_ids
):
    tokens, channels = ssm_inputs.shape
    heads = decay_rate.shape[0]
    state = state_write.shape[1]
    cols = channels // 2
    devices = lax.axis_size("seq")
    rows = devices // ROW
    send = lambda x, route: lax.ppermute(x, "seq", [(i, route(i)) for i in range(devices)])
    swap_c = lambda i: i ^ 1
    swap_y = lambda i: i ^ 2
    up = lambda n: lambda i: (i + n * ROW) % devices
    climb = lambda x, n=1: lax.ppermute(
        x, "seq", [(i, i + n * ROW) for i in range(devices - n * ROW)]
    )
    kv_width = keys_values.shape[2]
    half = cols // 2

    own, docs, mine, to_c, rates = call(
        pack_kernel,
        "pack",
        1.5,
        [
            ssm_inputs,
            state_write,
            state_read,
            decay_codes.T,
            keys_values,
            segment_ids[None, :],
            decay_rate[None, :],
        ],
        (
            shaped(2 * tokens + 16, kv_width),
            shaped(tokens, tokens, dtype=F32),
            shaped(tokens, cols + 2 * state + 128),
            shaped(tokens, cols + 2 * state + 128),
            shaped(1, 128, dtype=F32),
        ),
        [
            VMEM((heads, tokens), jnp.int32),
            VMEM((1, tokens), jnp.int32),
            VMEM((1, heads), F32),
            pltpu.SemaphoreType.DMA((11,)),
        ],
        True,
    )
    from_c = send(to_c, swap_c)
    behind2 = send(own, up(1))
    partner = send(own, swap_c)

    tail, tail_out, early, run, run_t, blocks = call(
        functools.partial(states_kernel, heads // 2, state),
        "states",
        2.0,
        [mine, from_c, rates],
        (
            shaped(state + LOGS, half),
            shaped(state + LOGS, half),
            shaped(state, cols),
            shaped(2, tokens, 128, dtype=F32),
            shaped(2, 128, tokens, dtype=F32),
            shaped(2, tokens, cols + 2 * state + 128),
        ),
        [VMEM((state + LOGS, cols), BF16)],
    )
    tail_y = send(tail_out, swap_y)
    carry = attend(
        after(queries, tail), docs, [own, partner], ((0, False), (0, True)), None, False
    )
    mixed = call(
        functools.partial(local_kernel, heads // 2, state),
        "local",
        0.01,
        [after(blocks, carry[1]), early, run, run_t],
        shaped(2, tokens, cols, dtype=F32),
    )
    tail_y = after(tail_y, mixed)
    span, first = call(
        functools.partial(row_kernel, state),
        "row",
        20.0,
        [tail, tail_y],
        (shaped(state + LOGS, half),) * 2,
    )
    new = send(span, up(1))
    behind2 = after(behind2, span)
    to_y = call(pick, "pick", 20.0, [own, behind2], shaped(2 * tokens + 16, kv_width))
    behind1 = send(to_y, swap_y)
    behind4 = send(after(behind2, to_y), up(1))
    behind2c = send(behind2, swap_c)
    before = None
    distance = 1
    while distance < rows:
        last = 2 * distance >= rows
        out = call(
            functools.partial(hop_kernel, state, distance, last),
            "hop%d" % distance,
            20.0,
            [span] + [before] * (distance > 1) + [new] + [first] * last,
            (shaped(state, half) if last else shaped(state + LOGS, half),) * 2,
        )
        if last:
            keep, give = out
        else:
            span, before = out
            new = climb(span, 2 * distance)
        if distance == 1:
            carry = attend(
                after(queries, before),
                docs,
                [behind2, behind2c],
                ((2, False), (2, True)),
                carry,
                False,
            )
            behind4, behind1 = after(behind4, carry[1]), after(behind1, carry[1])
            behind1c = send(behind1, swap_c)
            behind3 = send(behind1, up(1))
            behind4c = send(behind4, swap_c)
            new = after(new, carry[1])
        distance *= 2
    carry = attend(
        after(queries, give),
        docs,
        [behind1, behind1c, behind4, behind4c],
        ((1, False), (1, True), (4, False), (4, True)),
        carry,
        False,
    )
    behind3 = after(behind3, carry[1])
    behind3c = send(behind3, swap_c)
    other_half = after(send(give, swap_y), carry[1])
    done, for_c = call(
        functools.partial(finish_kernel, heads // 2, state),
        "finish",
        1.7,
        [mixed, run, blocks, keep, other_half],
        (shaped(tokens, cols),) * 2,
    )
    back_c = send(for_c, swap_c)
    attn_output = attend(
        after(queries, for_c),
        docs,
        [behind3, behind3c],
        ((3, False), (3, True)),
        carry,
        True,
    )
    ssm_output = call(
        collect_kernel,
        "collect",
        0.8,
        [done, after(back_c, attn_output)],
        shaped(tokens, channels),
    )
    return (ssm_output, attn_output)


def solution(mesh):
    return jax.shard_map(
        shards,
        mesh=mesh,
        in_specs=(
            P(("groups", "seq"), None),
            P(("groups", "seq"), None),
            P(("groups", "seq"), None),
            P(("groups", "seq"), None),
            P(),
            P(None, ("groups", "seq"), None),
            P(None, ("groups", "seq"), None),
            P(("groups", "seq")),
        ),
        out_specs=(P(("groups", "seq"), None), P(None, ("groups", "seq"), None)),
        check_vma=False,
    )
```

```python
import functools
import math

import jax
import jax.numpy as jnp
from jax import lax
from jax.experimental import pallas as pl
from jax.experimental.pallas import tpu as pltpu
from jax.sharding import PartitionSpec as P

KV_HEADS = 4
HEAD = 128
ROW = 4
FAR = -1e30
SCALE = HEAD ** (-0.5) * math.log2(math.e)
F32 = jnp.float32
BF16 = jnp.bfloat16
VMEM = pltpu.VMEM
IN_VMEM = pl.BlockSpec(memory_space=pltpu.VMEM)
LOGS = 16


def nt_dot(a, b):
    return lax.dot_general(a, b, (((1,), (1,)), ((), ())), preferred_element_type=F32)


def tn_dot(a, b, precision=None):
    return lax.dot_general(
        a, b, (((0,), (0,)), ((), ())), preferred_element_type=F32, precision=precision
    )


def lanes(number, width):
    return pl.ds(pl.multiple_of(number * width, width), width)


def call(kernel, name, micros, args, outs, scratch=(), stay=False, mib=8, leaves=False):
    out_spec = pl.BlockSpec(memory_space=pltpu.HBM) if leaves else IN_VMEM
    spec = pl.BlockSpec(memory_space=pltpu.HBM) if stay else IN_VMEM

    def placed(*refs):
        rank = lax.axis_index("seq")
        kernel((rank & 1, (rank >> 1) & 1, rank >> 2, rank >> 1), *refs)

    return pl.pallas_call(
        placed,
        name=name,
        out_shape=outs,
        in_specs=[spec] * len(args),
        out_specs=jax.tree.map(lambda _: out_spec, outs),
        scratch_shapes=list(scratch),
        cost_estimate=pl.CostEstimate(
            flops=int(micros * 1.15e9), bytes_accessed=0, transcendentals=0
        ),
        compiler_params=pltpu.CompilerParams(vmem_limit_bytes=mib * 1024 * 1024),
    )(*[pltpu.with_memory_space_constraint(a, pltpu.HBM) if stay else a for a in args])


def shaped(*shape, dtype=BF16):
    return jax.ShapeDtypeStruct(shape, dtype)


def pack_kernel(
    place, x, write, read, codes, kv, seg, rate, own, docs, mine, to_c, rates, code_buf, seg_buf, rate_buf,
    sems
):
    core = place[0]
    tokens, state = write.shape
    heads = codes.shape[0]
    half = x.shape[1] // 2
    copies = [
        (codes, code_buf),
        (seg, seg_buf),
        (rate, rate_buf),
        (kv.at[0], own.at[0:tokens]),
        (kv.at[1], own.at[tokens : 2 * tokens]),
        (x.at[:, lanes(1 - core, half)], to_c.at[:, 0:half]),
        (write, to_c.at[:, half : half + state]),
        (read, to_c.at[:, half + state : half + 2 * state]),
        (x.at[:, lanes(core, half)], mine.at[:, 0:half]),
        (write, mine.at[:, half : half + state]),
        (read, mine.at[:, half + state : half + 2 * state]),
    ]
    copies = [
        pltpu.make_async_copy(source, target, sems.at[n])
        for n, (source, target) in enumerate(copies)
    ]
    for copy in copies:
        copy.start()
    own[2 * tokens :, tokens:] = jnp.zeros((16, own.shape[1] - tokens), BF16)
    for copy in copies[:3]:
        copy.wait()
    codes_of = (seg_buf[...] + 1).astype(F32).astype(BF16)
    own[2 * tokens :, 0:tokens] = jnp.broadcast_to(codes_of, (16, tokens))
    docs[...] = jnp.transpose(jnp.broadcast_to(codes_of.astype(F32), (tokens, tokens)))
    code = code_buf[...]
    high = (code >> 6).astype(F32)
    low = (code & 63).astype(F32)
    gap = jnp.zeros((64 - heads, tokens), F32)
    both = jnp.transpose(jnp.concatenate([high, gap, low, gap], axis=0)).astype(BF16)
    mine[:, half + 2 * state :] = both
    to_c[:, half + 2 * state :] = both
    rates[...] = jnp.concatenate([rate_buf[...], jnp.zeros((1, 128 - heads), F32)], axis=1)
    for copy in copies[3:]:
        copy.wait()


def attend_kernel(kinds, first, last, place, q_ref, doc_ref, *refs):
    count = len(kinds)
    rows = q_ref.shape[1]
    pieces = refs[:count]
    at = count
    if not first:
        acc_in, peak_in, sum_in = refs[at : at + 3]
        at += 3
    if last:
        out_ref = refs[at]
        at += 1
    else:
        acc_out, peak_out, sum_out = refs[at : at + 3]
        at += 3
    bias = refs[at]
    core = place[0]
    chip = place[3]
    group = q_ref.shape[2] // HEAD // KV_HEADS
    if last:
        final_ref = out_ref
        out_ref, sems = refs[at + 1 :]

    def leave(head):
        cols = slice(head * group * HEAD, (head + 1) * group * HEAD)
        return pltpu.make_async_copy(
            out_ref.at[:, :, cols], final_ref.at[:, :, cols], sems.at[head]
        )

    def over_heads(body):
        for head in range(KV_HEADS):
            tiles = [
                (layer, slice((head * group + r) * HEAD, (head * group + r + 1) * HEAD))
                for layer in range(2)
                for r in range(group)
            ]
            body(head, [tiles[n : n + 2] for n in range(0, len(tiles), 2)])
            if last:
                leave(head).start()
        if last:
            for head in range(KV_HEADS):
                leave(head).wait()

    def stack(ref, pair):
        return jnp.concatenate([ref[layer, :, cols] for layer, cols in pair], axis=0)

    def unstack(ref, pair, value):
        for n, (layer, cols) in enumerate(pair):
            ref[layer, :, cols] = value[n * rows : (n + 1) * rows]

    def visit(here):
        mine = doc_ref[...]
        i = lax.broadcasted_iota(jnp.int32, (rows, rows), 0)
        j = lax.broadcasted_iota(jnp.int32, (rows, rows), 1)
        for n, (behind, other) in enumerate(kinds[:here]):
            theirs = pieces[n][2 * rows : 2 * rows + 16, 0:rows].astype(F32)[0:1]
            ok = theirs == mine
            if behind == 0 and not other:
                ok = ok & (j <= i)
            elif behind == 0:
                ok = ok & (j < rows * core)
            elif behind == 4 and not other:
                ok = ok & (j > i)
            elif behind == 4:
                ok = ok & (j < rows * (1 - core))
            bias[:, n * rows : (n + 1) * rows] = jnp.where(ok, 0.0, FAR)
        span = slice(0, here * rows)
        ones = jnp.ones((rows, HEAD), BF16)

        def body(head, pairs):
            cols = slice(head * HEAD, (head + 1) * HEAD)
            keys = jnp.concatenate([piece[0:rows, cols] for piece in pieces[:here]], axis=0)
            values = jnp.concatenate(
                [
                    jnp.concatenate([piece[rows : 2 * rows, cols], ones], axis=1)
                    for piece in pieces[:here]
                ],
                axis=0,
            )
            for pair in pairs:
                scores = nt_dot(stack(q_ref, pair), keys) * SCALE
                scores = scores + jnp.concatenate([bias[:, span]] * 2, axis=0)
                peak = jnp.max(scores, axis=1, keepdims=True)
                if first:
                    probs = jnp.exp2(scores - peak)
                else:
                    old = stack(peak_in, pair)
                    peak = jnp.maximum(old, peak)
                    fade = jnp.exp2(old - peak)
                    probs = jnp.concatenate(
                        [
                            jnp.exp2(scores[:, n * rows : (n + 1) * rows] - peak)
                            for n in range(here)
                        ],
                        axis=1,
                    )
                both = jnp.dot(probs.astype(BF16), values, preferred_element_type=F32)
                acc = both[:, :HEAD]
                total = both[:, HEAD:]
                if not first:
                    acc = acc + fade * stack(acc_in, pair)
                    total = total + fade * stack(sum_in, pair)
                if last:
                    unstack(out_ref, pair, (acc / total).astype(BF16))
                else:
                    unstack(acc_out, pair, acc)
                    unstack(sum_out, pair, total)
                    unstack(peak_out, pair, jnp.broadcast_to(peak, acc.shape))

        over_heads(body)

    def skip():
        def body(head, pairs):
            for pair in pairs:
                for layer, cols in pair:
                    out_ref[layer, :, cols] = (
                        acc_in[layer, :, cols] / sum_in[layer, :, cols]
                    ).astype(BF16)

        if last:
            over_heads(body)
        else:
            acc_out[...] = acc_in[...]
            sum_out[...] = sum_in[...]
            peak_out[...] = peak_in[...]

    steps = sorted({behind for behind, _ in kinds})
    for n, behind in enumerate(steps):
        here = sum(other <= behind for other, _ in kinds)
        enough = chip >= behind
        if n + 1 < len(steps):
            enough = enough & (chip < steps[n + 1])
        if behind == 0:
            visit(here)
        else:
            pl.when(enough)(functools.partial(visit, here))
    if not first:
        pl.when(chip < steps[0])(skip)


def attend(queries, docs, pieces, kinds, carry, last):
    layers, tokens, width = queries.shape
    count = len(kinds)
    partial = shaped(layers, tokens, width, dtype=F32)
    args = [queries, docs] + list(pieces) + list(carry or ())
    outs = shaped(layers, tokens, width) if last else (partial,) * 3
    return call(
        functools.partial(attend_kernel, kinds, carry is None, last),
        "attend%d" % kinds[-1][0],
        0.5 + 1.05 * count,
        args,
        outs,
        [
            VMEM((tokens, count * tokens), F32),
        ]
        + ([VMEM(queries.shape, BF16), pltpu.SemaphoreType.DMA((KV_HEADS,))] if last else []),
        mib=20,
        leaves=last,
    )


def spread(columns, pairs, width):
    low = lax.broadcasted_iota(jnp.int32, (1, 2 * width), 1) < width
    parts = [
        jnp.where(low, columns[:, 2 * k : 2 * k + 1], columns[:, 2 * k + 1 : 2 * k + 2])
        for k in range(pairs)
    ]
    return jnp.concatenate(parts, axis=1)


def put_logs(ref, state, logs):
    one = logs.astype(BF16)
    rest = logs - one.astype(F32)
    two = rest.astype(BF16)
    three = (rest - two.astype(F32)).astype(BF16)
    row = lax.broadcasted_iota(jnp.int32, (LOGS, logs.shape[1]), 0)
    ref[state:, :] = jnp.where(row == 0, one, jnp.where(row == 1, two, three))


def get_logs(ref, state):
    parts = ref[state:, :].astype(F32)
    return parts[0:1] + parts[1:2] + parts[2:3]


def states_kernel(
    heads, state, place, own_ref, c_ref, rate_ref, mine_ref, give_ref, early_ref, run_ref, turn_ref,
    xs, tail
):
    tokens = own_ref.shape[0]
    cols = early_ref.shape[1]
    width = cols // heads
    core, y = place[0], place[1]
    xs[core] = own_ref[...]
    xs[1 - core] = c_ref[...]
    i = lax.broadcasted_iota(jnp.int32, (tokens, tokens), 0)
    j = lax.broadcasted_iota(jnp.int32, (tokens, tokens), 1)
    lower_ones = (j <= i).astype(F32)
    upper_ones = (i <= j).astype(F32)
    low = lax.broadcasted_iota(jnp.int32, (1, 2 * width), 1) < width
    rates = rate_ref[...]
    shift = lax.rem(128 - core * heads, 128)
    kept = None
    offset = None
    for b in range(2):
        write = xs[b, :, cols : cols + state]
        high = xs[b, :, cols + 2 * state :].astype(F32)
        little = pltpu.roll(high, 64, 1)
        level = jnp.floor(high * 0.0625)
        lower = high * 64.0 + little - 1024.0 * level
        step = -rates * (1.0 + lower * (1.0 / 128.0)) - 0.125 * level
        step = jnp.where(j < heads, pltpu.roll(step, shift, 1), 0.0)
        run = jnp.dot(
            lower_ones, step, preferred_element_type=F32, precision=lax.Precision.HIGHEST
        )
        run_ref[b] = run
        turn_ref[b] = tn_dot(step, upper_ones, lax.Precision.HIGHEST)
        end = run[tokens - 1 : tokens, :]
        offset = end if b == 0 else offset + end
        to_end = jnp.exp(end - run)
        scaled = []
        for pair in range(heads // 2):
            tile = xs[b, :, pair * 2 * width : (pair + 1) * 2 * width]
            weight = jnp.where(
                low, to_end[:, 2 * pair : 2 * pair + 1], to_end[:, 2 * pair + 1 : 2 * pair + 2]
            )
            scaled.append((weight * tile.astype(F32)).astype(BF16))
        added = tn_dot(write, jnp.concatenate(scaled, axis=1))
        if b == 0:
            kept = added
            early_ref[...] = kept.astype(BF16)
        else:
            kept = spread(jnp.exp(end), heads // 2, width) * kept + added
    tail[0:state, :] = kept.astype(BF16)
    put_logs(tail, state, spread(offset, heads // 2, width))
    mine_ref[...] = tail[:, lanes(y, cols // 2)]
    give_ref[...] = tail[:, lanes(1 - y, cols // 2)]


def local_kernel(heads, state, place, xs, early_ref, run_ref, turn_ref, mixed_ref):
    tokens = run_ref.shape[1]
    cols = mixed_ref.shape[2]
    width = cols // heads
    i = lax.broadcasted_iota(jnp.int32, (tokens, tokens), 0)
    j = lax.broadcasted_iota(jnp.int32, (tokens, tokens), 1)
    low = lax.broadcasted_iota(jnp.int32, (1, 2 * width), 1) < width
    for b in range(2):
        write = xs[b, :, cols : cols + state]
        read = xs[b, :, cols + state : cols + 2 * state]
        run = run_ref[b]
        inner = jnp.where(j <= i, nt_dot(read, write), 0.0)
        if b > 0:
            fade = jnp.exp(run)
            seen = jnp.dot(read, early_ref[...], preferred_element_type=F32)
        for pair in range(heads // 2):
            part = slice(pair * 2 * width, (pair + 1) * 2 * width)
            tile = xs[b, :, part]
            mixes = []
            for h in (2 * pair, 2 * pair + 1):
                gap = jnp.minimum(run[:, h : h + 1] - turn_ref[b, h : h + 1, :], 0.0)
                mixes.append((inner * jnp.exp(gap)).astype(BF16))
            zero = jnp.zeros_like(tile)
            stacked = jnp.concatenate(
                [jnp.where(low, tile, zero), jnp.where(low, zero, tile)], axis=0
            )
            mixed = jnp.dot(jnp.concatenate(mixes, axis=1), stacked, preferred_element_type=F32)
            if b > 0:
                mixed = mixed + seen[:, part] * jnp.where(
                    low, fade[:, 2 * pair : 2 * pair + 1], fade[:, 2 * pair + 1 : 2 * pair + 2]
                )
            mixed_ref[b, :, part] = mixed


def pick(place, low_ref, high_ref, out_ref):
    @pl.when(place[1] == 0)
    def _():
        out_ref[...] = low_ref[...]

    @pl.when(place[1] != 0)
    def _():
        out_ref[...] = high_ref[...]


def row_kernel(state, place, tail_ref, y_ref, span_ref, first_ref):
    first = place[1] == 0
    mine = tail_ref[0:state, :].astype(F32)
    theirs = y_ref[0:state, :].astype(F32)
    my_log = get_logs(tail_ref, state)
    their_log = get_logs(y_ref, state)
    later = jnp.where(first, theirs, mine)
    earlier = jnp.where(first, mine, theirs)
    decay = jnp.exp(jnp.where(first, their_log, my_log))
    span_ref[0:state, :] = (later + decay * earlier).astype(BF16)
    put_logs(span_ref, state, my_log + their_log)
    first_ref[...] = jnp.where(first, tail_ref[...].astype(F32), y_ref[...].astype(F32)).astype(BF16)


def join(state, old_ref, new, new_logs):
    if old_ref is None:
        return new, new_logs
    logs = get_logs(old_ref, state)
    return old_ref[0:state, :].astype(F32) + jnp.exp(logs) * new, logs + new_logs


def hop_kernel(state, distance, last, place, *refs):
    refs = list(refs)
    span_ref = refs.pop(0)
    before_ref = refs.pop(0) if distance > 1 else None
    new_ref = refs.pop(0)
    ok = place[2] >= distance
    new = jnp.where(ok, new_ref[0:state, :].astype(F32), 0.0)
    new_logs = jnp.where(ok, get_logs(new_ref, state), 0.0)
    before, before_logs = join(state, before_ref, new, new_logs)
    if last:
        first_ref, keep_ref, give_ref = refs
        second, _ = join(state, first_ref, before, before_logs)
        y = place[1]
        keep_ref[...] = jnp.where(y == 0, before, second).astype(BF16)
        give_ref[...] = jnp.where(y == 0, second, before).astype(BF16)
    else:
        span_out, before_out = refs
        span, span_logs = join(state, span_ref, new, new_logs)
        span_out[0:state, :] = span.astype(BF16)
        put_logs(span_out, state, span_logs)
        before_out[0:state, :] = before.astype(BF16)
        put_logs(before_out, state, before_logs)


def finish_kernel(
    heads, state, place, mixed_ref, run_ref, xs, mine_ref, other_ref, self_ref, c_ref
):
    core = place[0]
    y = place[1]
    cols = mixed_ref.shape[2]
    width = cols // heads
    mine = mine_ref[...]
    other = other_ref[...]
    entering = jnp.concatenate(
        [jnp.where(y == 0, mine, other), jnp.where(y == 0, other, mine)], axis=1
    )
    a = lax.broadcasted_iota(jnp.int32, (4 * width, 2 * width), 0)
    b = lax.broadcasted_iota(jnp.int32, (4 * width, 2 * width), 1)
    same = (lax.rem(a, 2 * width) < width) == (b < width)
    average = jnp.where(same, 1.0 / width, 0.0).astype(BF16)
    low = lax.broadcasted_iota(jnp.int32, (1, 2 * width), 1) < width
    for out_ref, at in ((c_ref, 1 - core), (self_ref, core)):
        read = xs[at, :, cols + state : cols + 2 * state]
        seen = jnp.dot(read, entering, preferred_element_type=F32)
        ahead = jnp.where(at == 0, 0.0, run_ref[0, run_ref.shape[1] - 1 :, :])
        fade = jnp.exp(run_ref[at] + ahead)
        for pair in range(heads // 2):
            part = slice(pair * 2 * width, (pair + 1) * 2 * width)
            tile = mixed_ref[at, :, part] + seen[:, part] * jnp.where(
                low, fade[:, 2 * pair : 2 * pair + 1], fade[:, 2 * pair + 1 : 2 * pair + 2]
            )
            square = tile * tile
            big = square.astype(BF16)
            small = (square - big.astype(F32)).astype(BF16)
            mean = jnp.dot(
                jnp.concatenate([big, small], axis=1), average, preferred_element_type=F32
            )
            out_ref[:, part] = (tile * lax.rsqrt(mean + 1e-05)).astype(BF16)


def collect_kernel(place, self_ref, c_ref, out_ref, sems):
    core = place[0]
    cols = self_ref.shape[1]
    copies = [
        pltpu.make_async_copy(self_ref, out_ref.at[:, lanes(core, cols)], sems.at[0]),
        pltpu.make_async_copy(c_ref, out_ref.at[:, lanes(1 - core, cols)], sems.at[1]),
    ]
    for copy in copies:
        copy.start()
    for copy in copies:
        copy.wait()


def after(value, *others):
    return lax.optimization_barrier((value, *others))[0]


def shards(
    ssm_inputs, state_write, state_read, decay_codes, decay_rate, queries, keys_values, segment_ids
):
    tokens, channels = ssm_inputs.shape
    heads = decay_rate.shape[0]
    state = state_write.shape[1]
    cols = channels // 2
    devices = lax.axis_size("seq")
    rows = devices // ROW
    send = lambda x, route: lax.ppermute(x, "seq", [(i, route(i)) for i in range(devices)])
    swap_c = lambda i: i ^ 1
    swap_y = lambda i: i ^ 2
    up = lambda n: lambda i: (i + n * ROW) % devices
    climb = lambda x, n=1: lax.ppermute(
        x, "seq", [(i, i + n * ROW) for i in range(devices - n * ROW)]
    )
    kv_width = keys_values.shape[2]
    half = cols // 2

    own, docs, mine, to_c, rates = call(
        pack_kernel,
        "pack",
        1.5,
        [
            ssm_inputs,
            state_write,
            state_read,
            decay_codes.T,
            keys_values,
            segment_ids[None, :],
            decay_rate[None, :],
        ],
        (
            shaped(2 * tokens + 16, kv_width),
            shaped(tokens, tokens, dtype=F32),
            shaped(tokens, cols + 2 * state + 128),
            shaped(tokens, cols + 2 * state + 128),
            shaped(1, 128, dtype=F32),
        ),
        [
            VMEM((heads, tokens), jnp.int32),
            VMEM((1, tokens), jnp.int32),
            VMEM((1, heads), F32),
            pltpu.SemaphoreType.DMA((11,)),
        ],
        True,
    )
    from_c = send(to_c, swap_c)
    behind2 = send(own, up(1))
    partner = send(own, swap_c)

    tail, tail_out, early, run, run_t, blocks = call(
        functools.partial(states_kernel, heads // 2, state),
        "states",
        2.0,
        [mine, from_c, rates],
        (
            shaped(state + LOGS, half),
            shaped(state + LOGS, half),
            shaped(state, cols),
            shaped(2, tokens, 128, dtype=F32),
            shaped(2, 128, tokens, dtype=F32),
            shaped(2, tokens, cols + 2 * state + 128),
        ),
        [VMEM((state + LOGS, cols), BF16)],
    )
    tail_y = send(tail_out, swap_y)
    carry = attend(
        after(queries, tail), docs, [own, partner], ((0, False), (0, True)), None, False
    )
    mixed = call(
        functools.partial(local_kernel, heads // 2, state),
        "local",
        0.01,
        [after(blocks, carry[1]), early, run, run_t],
        shaped(2, tokens, cols, dtype=F32),
    )
    tail_y = after(tail_y, mixed)
    span, first = call(
        functools.partial(row_kernel, state),
        "row",
        20.0,
        [tail, tail_y],
        (shaped(state + LOGS, half),) * 2,
    )
    new = send(span, up(1))
    behind2 = after(behind2, span)
    to_y = call(pick, "pick", 20.0, [own, behind2], shaped(2 * tokens + 16, kv_width))
    behind1 = send(to_y, swap_y)
    behind4 = send(behind2, up(1))
    behind2c = send(behind2, swap_c)
    before = None
    distance = 1
    while distance < rows:
        last = 2 * distance >= rows
        out = call(
            functools.partial(hop_kernel, state, distance, last),
            "hop%d" % distance,
            20.0,
            [span] + [before] * (distance > 1) + [new] + [first] * last,
            (shaped(state, half) if last else shaped(state + LOGS, half),) * 2,
        )
        if last:
            keep, give = out
        else:
            span, before = out
            new = climb(span, 2 * distance)
        if distance == 1:
            carry = attend(
                after(queries, before),
                docs,
                [behind2, behind2c],
                ((2, False), (2, True)),
                carry,
                False,
            )
            behind4, behind1 = after(behind4, carry[1]), after(behind1, carry[1])
            behind1c = send(behind1, swap_c)
            behind3 = send(behind1, up(1))
            behind4c = send(behind4, swap_c)
            new = after(new, carry[1])
        distance *= 2
    carry = attend(
        after(queries, give),
        docs,
        [behind1, behind1c, behind4, behind4c],
        ((1, False), (1, True), (4, False), (4, True)),
        carry,
        False,
    )
    behind3 = after(behind3, carry[1])
    behind3c = send(behind3, swap_c)
    other_half = after(send(give, swap_y), carry[1])
    done, for_c = call(
        functools.partial(finish_kernel, heads // 2, state),
        "finish",
        1.7,
        [mixed, run, blocks, keep, other_half],
        (shaped(tokens, cols),) * 2,
    )
    back_c = send(for_c, swap_c)
    attn_output = attend(
        after(queries, for_c),
        docs,
        [behind3, behind3c],
        ((3, False), (3, True)),
        carry,
        True,
    )
    ssm_output = call(
        collect_kernel,
        "collect",
        0.8,
        [done, after(back_c, attn_output)],
        shaped(tokens, channels),
        [pltpu.SemaphoreType.DMA((2,))],
        leaves=True,
    )
    return (ssm_output, attn_output)


def solution(mesh):
    return jax.shard_map(
        shards,
        mesh=mesh,
        in_specs=(
            P(("groups", "seq"), None),
            P(("groups", "seq"), None),
            P(("groups", "seq"), None),
            P(("groups", "seq"), None),
            P(),
            P(None, ("groups", "seq"), None),
            P(None, ("groups", "seq"), None),
            P(("groups", "seq")),
        ),
        out_specs=(P(("groups", "seq"), None), P(None, ("groups", "seq"), None)),
        check_vma=False,
    )
```
